512 devices in a mesh: rep: 16 (over z), shard: 32 (over y, x, core).
Axes of the slice: x: 4, y: 4, z: 16, core: 2. Of those that a mesh axis runs over, the one named last changes fastest.
Arguments:
- hidden_acts: bfloat16 [65536, 1024], P(('rep', 'shard')), may hold values from -6 to 6
- out_grads: bfloat16 [65536, 8192], P(('rep', 'shard')), may hold values from -0.09375 to 0.09375
- momentum: float32 [16, 1024, 8192], P('rep', None, 'shard'), may hold values from -6 to 6
- kept: int32 [32], replicated, may hold values from 0 to 4095, as said below
Outputs:
- residual_momentum: float32 [16, 1024, 8192], P('rep', None, 'shard')
- update: bfloat16 [1024, 8192], P(None, 'shard')
The draws below stay inside these ranges and needn't reach their ends.
Inputs may be any that keep to these rules, and one draw needn't show every extreme that they name: `kept`: 32 distinct indices u * 64 + v of a block's coefficients, u the row frequency and v the column frequency; the same list for every block.
All inputs are finite; a program needn't handle non-finite values.
Results may differ from the reference program's by a relative error of at most 0.001.
Values may be sent and summed in bfloat16 or wider, within the bound.
No kernel may reach another device: no remote copies, remote signals or barrier semaphores. Data moves between devices by JAX's collectives and lax.ppermute only.
A program may use at most 64 MiB of HBM per device.

```python
import math
import jax
import jax.numpy as jnp
from jax import lax

D = 8192
ROWS = 1024
TOK_DEV = 128
GROUP = 64
KEPT = 32
TOKENS = 65536
REPLICAS = 16
N_REP = 16
N_SHARD = 32


def draw_kept(key, part):
    key = jax.random.fold_in(key, 7)
    first_key, second_key = jax.random.split(key)
    middle = jax.random.permutation(first_key, GROUP * GROUP - 2)[:KEPT - 2].astype(jnp.int32) + 1
    values = jnp.concatenate([jnp.zeros((1,), jnp.int32), middle, jnp.full((1,), GROUP * GROUP - 1, jnp.int32)])
    order = jax.random.permutation(second_key, KEPT)
    return values[order]


def levels(own_key, shape, cuts, low, largest):
    loudness = 1.0
    for dim, shards_of in cuts:
        steps = jax.random.uniform(jax.random.fold_in(jax.random.fold_in(own_key, 6), dim), (shards_of,), jnp.float32, low / len(cuts), largest / len(cuts))
        loudness = loudness * jnp.repeat(jnp.exp(steps), shape[dim] // shards_of).reshape((-1,) + (1,) * (len(shape) - 1 - dim))
    return loudness


def centred(stream_key, dims, spread, bound, cuts=(), held_as=jnp.bfloat16):
    array = spread * jax.random.normal(stream_key, dims, jnp.float32)
    if cuts:
        array = array * levels(stream_key, dims, cuts, -0.22, 0.18)
    return jnp.clip(array, -bound, bound).astype(held_as)


def setup_inputs(seed: int = 0) -> dict:
    seeds = jax.random.split(jax.random.key(seed), 5)
    return {
        "hidden_acts": centred(seeds[0], (TOKENS, ROWS), 1.0, 6.0, ((0, 512),)),
        "out_grads": centred(seeds[1], (TOKENS, D), (TOK_DEV * N_SHARD) ** -0.5, 0.09375, ((0, 512),)),
        "momentum": centred(seeds[2], (REPLICAS, ROWS, D), 1.0, 6.0, ((0, 16), (2, 32)), jnp.float32),
        "kept": draw_kept(jax.random.fold_in(seeds[4], 71), 0),
    }


decay_rate = 0.9

def cosine_matrix(length):
    frequency = jnp.arange(length, dtype=jnp.float32)[:, None]
    position = jnp.arange(length, dtype=jnp.float32)[None, :]
    cosines = jnp.cos(math.pi * (2.0 * position + 1.0) * frequency / (2.0 * length)) * math.sqrt(2.0 / length)
    return cosines * jnp.where(frequency == 0.0, math.sqrt(0.5), 1.0)

def reference(hidden_acts, out_grads, momentum, kept):
    cosines = cosine_matrix(GROUP)
    bands = ROWS // GROUP
    tiles = D // GROUP
    tok_rep = TOK_DEV * N_SHARD

    def to_blocks(field):
        return field.reshape(bands, GROUP, tiles, GROUP).transpose(0, 2, 1, 3)

    def from_blocks(blocks):
        return blocks.transpose(0, 2, 1, 3).reshape(ROWS, D)

    def extract(field):
        spectrum = jnp.einsum('un,abnm,vm->abuv', cosines, to_blocks(field), cosines, precision=lax.Precision.HIGHEST)
        return spectrum.reshape(bands, tiles, GROUP * GROUP)[:, :, kept]

    def restore(values):
        dense = jnp.zeros((bands, tiles, GROUP * GROUP), jnp.float32).at[:, :, kept].set(values)
        spatial = jnp.einsum('un,abuv,vm->abnm', cosines, dense.reshape(bands, tiles, GROUP, GROUP), cosines, precision=lax.Precision.HIGHEST)
        return from_blocks(spatial)

    def per_replica(index):
        acts = lax.dynamic_slice_in_dim(hidden_acts, index * tok_rep, tok_rep, 0)
        grads = lax.dynamic_slice_in_dim(out_grads, index * tok_rep, tok_rep, 0)
        gradient = jnp.dot(acts.T, grads, preferred_element_type=jnp.float32)
        fresh = decay_rate * momentum[index] + gradient
        values = extract(fresh)
        return (fresh - restore(values), values)
    residual, values = lax.map(per_replica, jnp.arange(N_REP, dtype=jnp.int32))
    update = restore(lax.optimization_barrier(jnp.sum(values, axis=0))).astype(jnp.bfloat16)
    return (residual, update)
```

```python
import functools
import math

import jax
import jax.numpy as jnp
from jax import lax
from jax.experimental import pallas as pl
from jax.experimental.pallas import tpu as pltpu
from jax.sharding import PartitionSpec as P

GROUP = 64
KEPT = 32
SIDE = 4
CHIPS = SIDE * SIDE
OFFSETS = (0, -1, 1, 2)

decay_rate = 0.9
f32 = jnp.float32
bf16 = jnp.bfloat16
HIGHEST = lax.Precision.HIGHEST
MIB = 1 << 20


def cosine(frequency, position):
    cosines = jnp.cos(
        math.pi * (2.0 * position + 1.0) * frequency / (2.0 * GROUP)
    ) * math.sqrt(2.0 / GROUP)
    return cosines * jnp.where(frequency == 0.0, math.sqrt(0.5), 1.0)


def dot(a, b, precision=None):
    return jnp.dot(a, b, preferred_element_type=f32, precision=precision)


def dot_nt(a, b, precision=None):
    return lax.dot_general(
        a, b, (((1,), (1,)), ((), ())), preferred_element_type=f32, precision=precision
    )


def whole(n):
    return [pl.BlockSpec(memory_space=pltpu.VMEM)] * n


def params(mib=48):
    return pltpu.CompilerParams(vmem_limit_bytes=mib * MIB)


def transpose_kernel(acts_ref, out_ref):
    out_ref[...] = acts_ref[...].astype(f32).T.astype(bf16)


def transposed(acts):
    tok, rows = acts.shape
    return pl.pallas_call(
        transpose_kernel,
        out_shape=jax.ShapeDtypeStruct((rows, tok), bf16),
        in_specs=whole(1),
        out_specs=pl.BlockSpec(memory_space=pltpu.VMEM),
        compiler_params=params(16),
    )(acts)


def split(a):
    high = a.astype(bf16)
    low = (a - high.astype(f32)).astype(bf16)
    return high, low


def coeff_kernel(acts_t_ref, grads_ref, left_ref, right_ref, out_ref, wide_ref, left_t_ref):
    rows, tok = acts_t_ref.shape
    bands = rows // GROUP
    groups, _, lanes = out_ref.shape
    columns = right_ref.shape[0]
    band = lax.broadcasted_iota(jnp.int32, (bands, 128), 0)
    lane = lax.broadcasted_iota(jnp.int32, (bands, 128), 1)
    for k in range(KEPT):
        row = jnp.broadcast_to(left_ref[k : k + 1, :], (bands, 128))
        for block in range(rows // 128):
            wide_ref[k * bands : (k + 1) * bands, block * 128 : (block + 1) * 128] = jnp.where(
                band == 2 * block + lane // GROUP, row, 0.0
            )
    wide = wide_ref[...]
    high, low = split(wide)
    lowest = (wide - high.astype(f32) - low.astype(f32)).astype(bf16)
    acts_t = acts_t_ref[...]
    left = dot(high, acts_t) + dot(low, acts_t) + dot(lowest, acts_t)
    high, low = split(left)
    left_t_ref[:, 0:tok] = high
    left_t_ref[:, tok : 2 * tok] = high
    left_t_ref[:, 2 * tok : 3 * tok] = low
    right = right_ref[...]
    r_high, r_low = split(right)
    r_lowest = (right - r_high.astype(f32) - r_low.astype(f32)).astype(bf16)
    kept_lane = lane % KEPT

    def one(g, carry):
        grads = grads_ref[:, pl.ds(pl.multiple_of(g * columns, columns), columns)]
        moved = dot(grads, r_high) + dot(grads, r_low) + dot(grads, r_lowest)
        high, low = split(moved)
        product = dot(left_t_ref[...], jnp.concatenate([high, low, high], axis=0))
        total = jnp.zeros((bands, lanes), f32)
        for k in range(KEPT):
            total = jnp.where(kept_lane == k, product[k * bands : (k + 1) * bands, :], total)
        out_ref[pl.ds(g, 1)] = total[None]
        return carry

    lax.fori_loop(0, groups, one, 0)


def local_coeffs(acts_t, grads, left_rows, right, groups):
    rows, tok = acts_t.shape
    bands = rows // GROUP
    lanes = right.shape[1]
    return pl.pallas_call(
        coeff_kernel,
        out_shape=jax.ShapeDtypeStruct((groups, bands, lanes), f32),
        in_specs=whole(4),
        out_specs=pl.BlockSpec(memory_space=pltpu.VMEM),
        scratch_shapes=[
            pltpu.VMEM((KEPT * bands, rows), f32),
            pltpu.VMEM((KEPT * bands, 3 * tok), bf16),
        ],
        compiler_params=params(),
        cost_estimate=pl.CostEstimate(flops=6 * 10**9, bytes_accessed=3 * MIB, transcendentals=0),
    )(acts_t, grads, left_rows, right)


def encode(field, left, right):
    rows = field.shape[0]
    moved = dot(field, right, HIGHEST)
    moved = moved.reshape(rows // GROUP, GROUP, right.shape[1]) * left[None]
    return jnp.sum(moved, axis=1)


def decode(coeffs, left, right):
    bands, lanes = coeffs.shape
    spread = (coeffs[:, None, :] * left[None]).reshape(bands * GROUP, lanes)
    return dot_nt(spread, right, HIGHEST)


def momentum_kernel(momentum_ref, coeffs_ref, left_ref, right_ref, out_ref):
    own = encode(decay_rate * momentum_ref[0], left_ref[...], right_ref[...])
    out_ref[...] = own + jnp.sum(coeffs_ref[...], axis=0)


def plane_coeffs(momentum, coeffs, left, right):
    return pl.pallas_call(
        momentum_kernel,
        out_shape=jax.ShapeDtypeStruct(coeffs.shape[1:], f32),
        in_specs=whole(4),
        out_specs=pl.BlockSpec(memory_space=pltpu.VMEM),
        compiler_params=params(),
        cost_estimate=pl.CostEstimate(flops=10**9, bytes_accessed=MIB, transcendentals=0),
    )(momentum, coeffs, left, right)


def update_kernel(coeffs_ref, left_ref, right_ref, out_ref):
    total = jnp.sum(coeffs_ref[...], axis=0)
    out_ref[...] = decode(total, left_ref[...], right_ref[...]).astype(bf16)


def decoded_update(coeffs, left, right, rows):
    return pl.pallas_call(
        update_kernel,
        out_shape=jax.ShapeDtypeStruct((rows, right.shape[0]), bf16),
        in_specs=whole(3),
        out_specs=pl.BlockSpec(memory_space=pltpu.VMEM),
        compiler_params=params(),
        cost_estimate=pl.CostEstimate(flops=10**9, bytes_accessed=MIB, transcendentals=0),
    )(coeffs, left, right)


def residual_kernel(momentum_ref, own_ref, other_ref, left_ref, right_ref, out_ref):
    fresh = decay_rate * momentum_ref[0] + (own_ref[...] + other_ref[...])
    left, right = left_ref[...], right_ref[...]
    out_ref[0] = fresh - decode(encode(fresh, left, right), left, right)


def residual_of(momentum, own, other, left, right):
    return pl.pallas_call(
        residual_kernel,
        out_shape=jax.ShapeDtypeStruct(momentum.shape, f32),
        in_specs=whole(5),
        out_specs=pl.BlockSpec(memory_space=pltpu.VMEM),
        compiler_params=params(),
        cost_estimate=pl.CostEstimate(flops=2 * 10**9, bytes_accessed=4 * MIB, transcendentals=0),
    )(momentum, own, other, left, right)


def product_kernel(place_ref, *refs):
    *acts_refs, grads_ref, out_ref = refs
    columns = out_ref.shape[1]
    start = pl.multiple_of(place_ref[CHIPS] * columns, columns)
    total = None
    for outer, acts_ref in enumerate(acts_refs):
        grads = jnp.concatenate(
            [
                grads_ref[place_ref[outer * SIDE + inner], :, pl.ds(start, columns)]
                for inner in range(SIDE)
            ],
            axis=0,
        )
        term = dot(acts_ref[...], grads)
        total = term if total is None else total + term
    out_ref[...] = total


def product(place, acts, grads):
    rows = acts[0].shape[0]
    columns = grads.shape[2] // 2
    return pl.pallas_call(
        product_kernel,
        out_shape=jax.ShapeDtypeStruct((rows, columns), f32),
        in_specs=[pl.BlockSpec(memory_space=pltpu.SMEM)] + whole(len(acts) + 1),
        out_specs=pl.BlockSpec(memory_space=pltpu.VMEM),
        compiler_params=params(),
        cost_estimate=pl.CostEstimate(flops=10**9, bytes_accessed=7 * MIB, transcendentals=0),
    )(place, *acts, grads)


def spot(y, x, core):
    return ((y % SIDE) * SIDE + x % SIDE) * 2 + core


def shifted(block, step, phase):
    pairs = []
    for y in range(SIDE):
        for x in range(SIDE):
            for core in range(2):
                along_x = core == phase
                to = spot(y, x + step, core) if along_x else spot(y + step, x, core)
                pairs.append((spot(y, x, core), to))
    return lax.ppermute(block, "shard", pairs)


def on_device(hidden_acts, out_grads, momentum, kept):
    tok, rows = hidden_acts.shape
    columns = momentum.shape[2]
    shards = out_grads.shape[1] // columns
    replicas = lax.axis_size("rep")
    lanes = columns // GROUP * KEPT
    me = lax.axis_index("shard").astype(jnp.int32)
    core, mine_x, mine_y = me % 2, me // 2 % SIDE, me // (2 * SIDE)

    acts_t = transposed(hidden_acts)
    first = jnp.concatenate([acts_t] + [shifted(acts_t, -d, 0) for d in OFFSETS[1:]], axis=1)
    gathered = [first] + [shifted(first, -d, 1) for d in OFFSETS[1:]]

    same_core = [[2 * chip + c for chip in range(CHIPS)] for c in range(2)]
    grads = out_grads.reshape(tok, CHIPS, 2 * columns).transpose(1, 0, 2)
    grads = lax.all_to_all(
        grads, "shard", split_axis=0, concat_axis=0, axis_index_groups=same_core, tiled=True
    )

    lane = jnp.arange(lanes, dtype=jnp.int32)
    row_frequency = (kept // GROUP).astype(f32)
    column_frequency = (kept % GROUP).astype(f32)
    position = jnp.arange(GROUP, dtype=f32)
    left = cosine(jnp.tile(row_frequency, lanes // KEPT)[None, :], position[:, None])
    left_rows = cosine(row_frequency[:, None], jnp.tile(position, 128 // GROUP)[None, :])
    right = jnp.tile(
        cosine(jnp.tile(column_frequency, lanes // KEPT)[None, :], position[:, None]),
        (columns // GROUP, 1),
    )
    block = jnp.arange(columns, dtype=jnp.int32)[:, None] // GROUP
    right = jnp.where(block == lane[None, :] // KEPT, right, 0.0)

    coeffs = local_coeffs(acts_t, out_grads, left_rows, right, shards)
    coeffs = lax.all_to_all(coeffs, "shard", split_axis=0, concat_axis=0, tiled=True)
    coeffs = plane_coeffs(momentum, coeffs, left, right)
    coeffs = lax.all_to_all(
        jnp.broadcast_to(coeffs[None], (replicas,) + coeffs.shape),
        "rep",
        split_axis=0,
        concat_axis=0,
        tiled=True,
    )
    update = decoded_update(coeffs, left, right, rows)

    shift = jnp.array(OFFSETS, jnp.int32)
    outer, inner = jnp.repeat(shift, SIDE), jnp.tile(shift, SIDE)
    x = (mine_x + jnp.where(core == 0, inner, outer)) % SIDE
    y = (mine_y + jnp.where(core == 0, outer, inner)) % SIDE
    place = y * SIDE + x

    other = product(jnp.concatenate([place, 1 - core[None]]), gathered, grads)
    own = product(jnp.concatenate([place, core[None]]), gathered, grads)
    swap = [(i, i ^ 1) for i in range(shards)]
    other = lax.ppermute(other, "shard", swap)
    residual = residual_of(momentum, own, other, left, right)
    return (residual, update)


def solution(mesh):
    placed = (P(("rep", "shard"), None), P(("rep", "shard"), None), P("rep", None, "shard"), P())
    return jax.shard_map(
        on_device,
        mesh=mesh,
        in_specs=placed,
        out_specs=(P("rep", None, "shard"), P(None, "shard")),
        check_vma=False,
    )
```

```python
import functools
import math

import jax
import jax.numpy as jnp
import numpy as np
from jax import lax
from jax.experimental import pallas as pl
from jax.experimental.pallas import tpu as pltpu
from jax.sharding import PartitionSpec as P

GROUP = 64
KEPT = 32
SIDE = 4
CHIPS = SIDE * SIDE
OFFSETS = (0, 2, 1, -1)

decay_rate = 0.9
f32 = jnp.float32
bf16 = jnp.bfloat16
HIGHEST = lax.Precision.HIGHEST
MIB = 1 << 20
COST = pl.CostEstimate(flops=0, bytes_accessed=0, transcendentals=0)


def dot(a, b, precision=None):
    return jnp.dot(a, b, preferred_element_type=f32, precision=precision)


def dot_nt(a, b, precision=None):
    return lax.dot_general(
        a, b, (((1,), (1,)), ((), ())), preferred_element_type=f32, precision=precision
    )


def whole(n):
    return [pl.BlockSpec(memory_space=pltpu.VMEM)] * n


def params(mib=48):
    return pltpu.CompilerParams(vmem_limit_bytes=mib * MIB)


def first_kernel(place_ref, acts_ref, grads_ref, *refs):
    tok, rows = acts_ref.shape
    width = refs[0].shape[1]
    depth = rows * tok // width
    half = width // 2
    core, near, far = place_ref[0], place_ref[1], place_ref[2]
    acts_t = acts_ref[...].astype(f32).T.astype(bf16)
    for q in range(width // tok):
        for ref in refs:
            ref[0:depth, q * tok : (q + 1) * tok] = acts_t[q * depth : (q + 1) * depth]
    for i, ref in enumerate(refs):
        a = (near + OFFSETS[i] + SIDE) % SIDE
        for j, d in enumerate(OFFSETS):
            b = (far + d + SIDE) % SIDE
            chip = jnp.where(core == 0, b * SIDE + a, a * SIDE + b)
            for h in range(2):
                start = pl.multiple_of(chip * width + (core + h) % 2 * half, half)
                ref[depth + j * tok : depth + (j + 1) * tok, h * half : (h + 1) * half] = grads_ref[
                    :, pl.ds(start, half)
                ]


def first_packets(place, acts, grads):
    tok, rows = acts.shape
    width = grads.shape[1] // CHIPS
    packet = jax.ShapeDtypeStruct((rows * tok // width + SIDE * tok, width), bf16)
    return pl.pallas_call(
        first_kernel,
        out_shape=(packet,) * SIDE,
        in_specs=[pl.BlockSpec(memory_space=pltpu.SMEM)] + whole(2),
        out_specs=tuple(whole(SIDE)),
        compiler_params=params(16),
        cost_estimate=COST,
    )(place, acts, grads)


def second_kernel(*refs):
    in_refs, out_refs = refs[:SIDE], refs[SIDE:]
    length, width = out_refs[0].shape
    tok = width // SIDE
    rows = length - SIDE * tok
    depth = rows * tok // width
    for i, ref in enumerate(in_refs):
        for q in range(SIDE):
            quarter = ref[0:depth, q * tok : (q + 1) * tok]
            for out_ref in out_refs:
                out_ref[q * depth : (q + 1) * depth, i * tok : (i + 1) * tok] = quarter
        for j, out_ref in enumerate(out_refs):
            out_ref[rows + i * tok : rows + (i + 1) * tok, :] = ref[
                depth + j * tok : depth + (j + 1) * tok, :
            ]


def second_packets(packets, rows):
    length, width = packets[0].shape
    packet = jax.ShapeDtypeStruct((rows + width, width), bf16)
    return pl.pallas_call(
        second_kernel,
        out_shape=(packet,) * SIDE,
        in_specs=whole(SIDE),
        out_specs=tuple(whole(SIDE)),
        compiler_params=params(16),
        cost_estimate=COST,
    )(*packets)


def split(a):
    high = a.astype(bf16)
    return high, (a - high.astype(f32)).astype(bf16)


def split3(a):
    high = a.astype(bf16)
    rest = a - high.astype(f32)
    middle = rest.astype(bf16)
    return high, middle, (rest - middle.astype(f32)).astype(bf16)


BATCH = 4


def coeff_kernel(lanes_ref, table_ref, acts_ref, grads_ref, out_ref, left_ref, right_ref, twice_ref):
    tok, rows = acts_ref.shape
    bands = rows // GROUP
    groups, _, lanes = out_ref.shape
    columns = right_ref.shape[0]

    frequency = lax.broadcasted_iota(jnp.int32, (GROUP, lanes), 0)
    table = table_ref[...]
    kept_lanes = lanes_ref[...]
    picked_row = jnp.where(frequency == kept_lanes // GROUP, 1.0, 0.0)
    picked_column = jnp.where(frequency == kept_lanes % GROUP, 1.0, 0.0)
    left = dot(table, picked_row, HIGHEST)
    tall = dot(table, picked_column, HIGHEST)
    left_ref[...] = left
    lane = lax.broadcasted_iota(jnp.int32, (GROUP, lanes), 1)
    right = jnp.concatenate(
        [jnp.where(lane // KEPT == b, tall, 0.0) for b in range(columns // GROUP)], axis=0
    )
    right_ref[...] = right
    pieces = jnp.concatenate(split(right), axis=1)

    acts_t = acts_ref[...].astype(f32).T.astype(bf16)
    twice_ref[:, 0:tok] = acts_t
    twice_ref[:, tok : 2 * tok] = acts_t

    def step(i, carry):
        start = pl.multiple_of(i * BATCH * columns, BATCH * columns)
        grads = jnp.concatenate(
            [grads_ref[:, pl.ds(start + j * columns, columns)] for j in range(BATCH)], axis=0
        )
        moved = dot(grads, pieces)
        high, low = split(moved[:, :lanes] + moved[:, lanes:])
        for j in range(0, BATCH, 2):
            both = [jnp.concatenate([p[m * tok : (m + 1) * tok] for p in (high, low)], axis=0) for m in (j, j + 1)]
            product = dot(twice_ref[...], jnp.concatenate(both, axis=1))
            for m in range(2):
                part = product[:, m * lanes : (m + 1) * lanes].reshape(bands, GROUP, lanes) * left[None]
                out_ref[pl.ds(i * BATCH + j + m, 1)] = jnp.sum(part, axis=1)[None]
        return carry

    lax.fori_loop(0, groups // BATCH, step, 0)


def local_coeffs(kept, acts, grads, columns):
    tok, rows = acts.shape
    bands = rows // GROUP
    lanes = columns // GROUP * KEPT
    frequency = np.arange(GROUP, dtype=np.float32)[None, :]
    position = np.arange(GROUP, dtype=np.float32)[:, None]
    table = np.cos(
        np.float32(math.pi) * (2.0 * position + 1.0) * frequency / np.float32(2.0 * GROUP)
    ) * np.float32(math.sqrt(2.0 / GROUP))
    table = (table * np.where(frequency == 0.0, math.sqrt(0.5), 1.0)).astype(np.float32)
    return pl.pallas_call(
        coeff_kernel,
        out_shape=(
            jax.ShapeDtypeStruct((grads.shape[1] // columns, bands, lanes), f32),
            jax.ShapeDtypeStruct((GROUP, lanes), f32),
            jax.ShapeDtypeStruct((columns, lanes), f32),
        ),
        in_specs=whole(4),
        out_specs=tuple(whole(3)),
        scratch_shapes=[pltpu.VMEM((rows, 2 * tok), bf16)],
        compiler_params=params(16),
        cost_estimate=COST,
    )(jnp.tile(kept, lanes // KEPT)[None, :], jnp.asarray(table), acts, grads)


def encode(field, left, right):
    rows = field.shape[0]
    high, low = split(field)
    r_high, r_low = split(right)
    moved = dot(high, r_high) + dot(low, r_high) + dot(high, r_low)
    moved = moved.reshape(rows // GROUP, GROUP, right.shape[1]) * left[None]
    return jnp.sum(moved, axis=1)


def decode(coeffs, left, right):
    bands, lanes = coeffs.shape
    spread = (coeffs[:, None, :] * left[None]).reshape(bands * GROUP, lanes)
    high, low = split(spread)
    r_high, r_low = split(right)
    return dot_nt(
        jnp.concatenate([high, low, high], axis=1),
        jnp.concatenate([r_high, r_high, r_low], axis=1),
    )


def momentum_kernel(momentum_ref, coeffs_ref, left_ref, right_ref, out_ref):
    own = encode(decay_rate * momentum_ref[0], left_ref[...], right_ref[...])
    out_ref[...] = own + jnp.sum(coeffs_ref[...], axis=0)


def plane_coeffs(momentum, coeffs, left, right):
    return pl.pallas_call(
        momentum_kernel,
        out_shape=jax.ShapeDtypeStruct(coeffs.shape[1:], f32),
        in_specs=whole(4),
        out_specs=pl.BlockSpec(memory_space=pltpu.VMEM),
        compiler_params=params(16),
        cost_estimate=COST,
    )(momentum, coeffs, left, right)


def update_kernel(coeffs_ref, left_ref, right_ref, out_ref):
    total = jnp.sum(coeffs_ref[...], axis=0)
    out_ref[...] = decode(total, left_ref[...], right_ref[...]).astype(bf16)


def decoded_update(coeffs, left, right, rows):
    return pl.pallas_call(
        update_kernel,
        out_shape=jax.ShapeDtypeStruct((rows, right.shape[0]), bf16),
        in_specs=whole(3),
        out_specs=pl.BlockSpec(memory_space=pltpu.VMEM),
        compiler_params=params(16),
        cost_estimate=COST,
    )(coeffs, left, right)


def term(ref, side, columns):
    rows = ref.shape[0] - ref.shape[1]
    return dot(ref[0:rows, :], ref[rows:, side * columns : (side + 1) * columns])


def terms(refs, side, columns):
    total = term(refs[0], side, columns)
    for ref in refs[1:]:
        total = total + term(ref, side, columns)
    return total


def other_kernel(*refs):
    *packet_refs, out_ref = refs
    out_ref[...] = terms(packet_refs, 1, out_ref.shape[1])


def other_product(packets):
    length, width = packets[0].shape
    return pl.pallas_call(
        other_kernel,
        out_shape=jax.ShapeDtypeStruct((length - width, width // 2), f32),
        in_specs=whole(len(packets)),
        out_specs=pl.BlockSpec(memory_space=pltpu.VMEM),
        compiler_params=params(16),
        cost_estimate=COST,
    )(*packets)


def fresh_kernel(*refs):
    *packet_refs, momentum_ref, out_ref = refs
    out_ref[...] = decay_rate * momentum_ref[0] + terms(packet_refs, 0, out_ref.shape[1])


def own_fresh(packets, momentum):
    return pl.pallas_call(
        fresh_kernel,
        out_shape=jax.ShapeDtypeStruct(momentum.shape[1:], f32),
        in_specs=whole(len(packets) + 1),
        out_specs=pl.BlockSpec(memory_space=pltpu.VMEM),
        compiler_params=params(16),
        cost_estimate=COST,
    )(*packets, momentum)


def residual_kernel(own_ref, other_ref, left_ref, right_ref, out_ref):
    fresh = own_ref[...] + other_ref[...]
    left, right = left_ref[...], right_ref[...]
    out_ref[0] = fresh - decode(encode(fresh, left, right), left, right)


def residual_of(own, other, left, right):
    return pl.pallas_call(
        residual_kernel,
        out_shape=jax.ShapeDtypeStruct((1,) + own.shape, f32),
        in_specs=whole(4),
        out_specs=pl.BlockSpec(memory_space=pltpu.VMEM),
        compiler_params=params(16),
        cost_estimate=COST,
    )(own, other, left, right)


def spot(y, x, core):
    return ((y % SIDE) * SIDE + x % SIDE) * 2 + core


def shifted(block, step, phase):
    pairs = []
    for y in range(SIDE):
        for x in range(SIDE):
            for core in range(2):
                along_x = core == phase
                to = spot(y, x + step, core) if along_x else spot(y + step, x, core)
                pairs.append((spot(y, x, core), to))
    return lax.ppermute(block, "shard", pairs)


def on_device(hidden_acts, out_grads, momentum, kept):
    tok, rows = hidden_acts.shape
    columns = momentum.shape[2]
    shards = out_grads.shape[1] // columns
    replicas = lax.axis_size("rep")
    me = lax.axis_index("shard").astype(jnp.int32)
    core, mine_x, mine_y = me % 2, me // 2 % SIDE, me // (2 * SIDE)

    place = jnp.stack([core, jnp.where(core == 0, mine_x, mine_y), jnp.where(core == 0, mine_y, mine_x)])
    packets = first_packets(place, hidden_acts, out_grads)
    packets = [packets[0]] + [shifted(p, d, 0) for p, d in zip(packets[1:], OFFSETS[1:])]

    coeffs, left, right = local_coeffs(kept, hidden_acts, out_grads, columns)

    coeffs = lax.all_to_all(coeffs, "shard", split_axis=0, concat_axis=0, tiled=True)
    coeffs, *packets = lax.optimization_barrier((coeffs, *packets))

    packets = second_packets(packets, rows)
    packets = [packets[0]] + [shifted(p, d, 1) for p, d in zip(packets[1:], OFFSETS[1:])]

    coeffs = plane_coeffs(momentum, coeffs, left, right)
    coeffs = lax.all_to_all(
        jnp.broadcast_to(coeffs[None], (replicas,) + coeffs.shape),
        "rep",
        split_axis=0,
        concat_axis=0,
        tiled=True,
    )
    coeffs, *packets = lax.optimization_barrier((coeffs, *packets))
    update = decoded_update(coeffs, left, right, rows)

    other = other_product(packets)
    swap = [(i, i ^ 1) for i in range(shards)]
    other = lax.ppermute(other, "shard", swap)
    own = own_fresh(packets, momentum)
    residual = residual_of(own, other, left, right)
    return (residual, update)


def solution(mesh):
    placed = (P(("rep", "shard"), None), P(("rep", "shard"), None), P("rep", None, "shard"), P())
    return jax.shard_map(
        on_device,
        mesh=mesh,
        in_specs=placed,
        out_specs=(P("rep", None, "shard"), P(None, "shard")),
        check_vma=False,
    )
```

```python
import functools
import math

import jax
import jax.numpy as jnp
import numpy as np
from jax import lax
from jax.experimental import pallas as pl
from jax.experimental.pallas import tpu as pltpu
from jax.sharding import PartitionSpec as P

GROUP = 64
KEPT = 32
SIDE = 4
CHIPS = SIDE * SIDE
OFFSETS = (0, 2, 1, -1)

decay_rate = 0.9
f32 = jnp.float32
bf16 = jnp.bfloat16
HIGHEST = lax.Precision.HIGHEST
MIB = 1 << 20
COST = pl.CostEstimate(flops=0, bytes_accessed=0, transcendentals=0)


def dot(a, b, precision=None):
    return jnp.dot(a, b, preferred_element_type=f32, precision=precision)


def dot_nt(a, b, precision=None):
    return lax.dot_general(
        a, b, (((1,), (1,)), ((), ())), preferred_element_type=f32, precision=precision
    )


def whole(n):
    return [pl.BlockSpec(memory_space=pltpu.VMEM)] * n


def params(mib=48):
    return pltpu.CompilerParams(vmem_limit_bytes=mib * MIB)


def first_kernel(place_ref, acts_hbm, grads_hbm, *refs):
    *out_refs, acts_ref, grads_ref, sems = refs
    copies = [
        pltpu.make_async_copy(acts_hbm, acts_ref, sems.at[0]),
        pltpu.make_async_copy(grads_hbm, grads_ref, sems.at[1]),
    ]
    for copy in copies:
        copy.start()
    tok, rows = acts_ref.shape
    width = out_refs[0].shape[1]
    depth = rows * tok // width
    half = width // 2
    core, near, far = place_ref[0], place_ref[1], place_ref[2]
    copies[0].wait()
    acts_t = acts_ref[...].astype(f32).T.astype(bf16)
    for q in range(width // tok):
        for ref in out_refs:
            ref[0:depth, q * tok : (q + 1) * tok] = acts_t[q * depth : (q + 1) * depth]
    copies[1].wait()
    for i, ref in enumerate(out_refs):
        a = (near + OFFSETS[i] + SIDE) % SIDE
        for j, d in enumerate(OFFSETS):
            b = (far + d + SIDE) % SIDE
            chip = jnp.where(core == 0, b * SIDE + a, a * SIDE + b)
            for h in range(2):
                start = pl.multiple_of(chip * width + (core + h) % 2 * half, half)
                ref[depth + j * tok : depth + (j + 1) * tok, h * half : (h + 1) * half] = grads_ref[
                    :, pl.ds(start, half)
                ]


def first_packets(place, acts, grads):
    tok, rows = acts.shape
    width = grads.shape[1] // CHIPS
    packet = jax.ShapeDtypeStruct((rows * tok // width + SIDE * tok, width), bf16)
    return pl.pallas_call(
        first_kernel,
        out_shape=(packet,) * SIDE,
        in_specs=[pl.BlockSpec(memory_space=pltpu.SMEM)]
        + [pl.BlockSpec(memory_space=pltpu.HBM)] * 2,
        out_specs=tuple(whole(SIDE)),
        scratch_shapes=[
            pltpu.VMEM(acts.shape, bf16),
            pltpu.VMEM(grads.shape, bf16),
            pltpu.SemaphoreType.DMA((2,)),
        ],
        compiler_params=params(16),
        cost_estimate=COST,
    )(place, *(pltpu.with_memory_space_constraint(a, pltpu.HBM) for a in (acts, grads)))


def second_kernel(*refs):
    in_refs, out_refs = refs[:SIDE], refs[SIDE:]
    length, width = out_refs[0].shape
    tok = width // SIDE
    rows = length - SIDE * tok
    depth = rows * tok // width
    for i, ref in enumerate(in_refs):
        for q in range(SIDE):
            quarter = ref[0:depth, q * tok : (q + 1) * tok]
            for out_ref in out_refs:
                out_ref[q * depth : (q + 1) * depth, i * tok : (i + 1) * tok] = quarter
        for j, out_ref in enumerate(out_refs):
            out_ref[rows + i * tok : rows + (i + 1) * tok, :] = ref[
                depth + j * tok : depth + (j + 1) * tok, :
            ]


def second_packets(packets, rows):
    length, width = packets[0].shape
    packet = jax.ShapeDtypeStruct((rows + width, width), bf16)
    return pl.pallas_call(
        second_kernel,
        out_shape=(packet,) * SIDE,
        in_specs=whole(SIDE),
        out_specs=tuple(whole(SIDE)),
        compiler_params=params(16),
        cost_estimate=COST,
    )(*packets)


def split(a):
    high = a.astype(bf16)
    return high, (a - high.astype(f32)).astype(bf16)


def split3(a):
    high = a.astype(bf16)
    rest = a - high.astype(f32)
    middle = rest.astype(bf16)
    return high, middle, (rest - middle.astype(f32)).astype(bf16)


BATCH = 8


def coeff_kernel(kept_ref, table_ref, acts_ref, grads_ref, out_ref, left_ref, right_ref, twice_ref):
    tok, rows = acts_ref.shape
    bands = rows // GROUP
    groups, _, lanes = out_ref.shape
    columns = right_ref.shape[0]

    frequency = lax.broadcasted_iota(jnp.int32, (GROUP, lanes), 0)
    table = table_ref[...]
    kept_lanes = jnp.concatenate([kept_ref[...]] * (lanes // KEPT), axis=1)
    picked_row = jnp.where(frequency == kept_lanes // GROUP, 1.0, 0.0)
    picked_column = jnp.where(frequency == kept_lanes % GROUP, 1.0, 0.0)
    left = dot(table, picked_row, HIGHEST)
    tall = dot(table, picked_column, HIGHEST)
    left_ref[...] = left
    lane = lax.broadcasted_iota(jnp.int32, (GROUP, lanes), 1)
    right = jnp.concatenate(
        [jnp.where(lane // KEPT == b, tall, 0.0) for b in range(columns // GROUP)], axis=0
    )
    right_ref[...] = right
    pieces = jnp.concatenate(split(right), axis=1)

    acts_t = acts_ref[...].astype(f32).T.astype(bf16)
    twice_ref[:, 0:tok] = acts_t
    twice_ref[:, tok : 2 * tok] = acts_t

    def step(i, carry):
        start = pl.multiple_of(i * BATCH * columns, BATCH * columns)
        grads = jnp.concatenate(
            [grads_ref[:, pl.ds(start + j * columns, columns)] for j in range(BATCH)], axis=0
        )
        moved = dot(grads, pieces)
        high, low = split(moved[:, :lanes] + moved[:, lanes:])
        for j in range(0, BATCH, 2):
            both = [jnp.concatenate([p[m * tok : (m + 1) * tok] for p in (high, low)], axis=0) for m in (j, j + 1)]
            product = dot(twice_ref[...], jnp.concatenate(both, axis=1))
            for m in range(2):
                part = product[:, m * lanes : (m + 1) * lanes].reshape(bands, GROUP, lanes) * left[None]
                out_ref[pl.ds(i * BATCH + j + m, 1)] = jnp.sum(part, axis=1)[None]
        return carry

    lax.fori_loop(0, groups // BATCH, step, 0)


def local_coeffs(kept, acts, grads, columns):
    tok, rows = acts.shape
    bands = rows // GROUP
    lanes = columns // GROUP * KEPT
    frequency = np.arange(GROUP, dtype=np.float32)[None, :]
    position = np.arange(GROUP, dtype=np.float32)[:, None]
    table = np.cos(
        np.float32(math.pi) * (2.0 * position + 1.0) * frequency / np.float32(2.0 * GROUP)
    ) * np.float32(math.sqrt(2.0 / GROUP))
    table = (table * np.where(frequency == 0.0, math.sqrt(0.5), 1.0)).astype(np.float32)
    return pl.pallas_call(
        coeff_kernel,
        out_shape=(
            jax.ShapeDtypeStruct((grads.shape[1] // columns, bands, lanes), f32),
            jax.ShapeDtypeStruct((GROUP, lanes), f32),
            jax.ShapeDtypeStruct((columns, lanes), f32),
        ),
        in_specs=whole(4),
        out_specs=tuple(whole(3)),
        scratch_shapes=[pltpu.VMEM((rows, 2 * tok), bf16)],
        compiler_params=params(16),
        cost_estimate=COST,
    )(kept[None, :], jnp.asarray(table), acts, grads)


def encode(field, left, right):
    rows = field.shape[0]
    high, low = split(field)
    r_high, r_low = split(right)
    moved = dot(high, r_high) + dot(low, r_high) + dot(high, r_low)
    moved = moved.reshape(rows // GROUP, GROUP, right.shape[1]) * left[None]
    return jnp.sum(moved, axis=1)


def decode(coeffs, left, right):
    bands, lanes = coeffs.shape
    spread = (coeffs[:, None, :] * left[None]).reshape(bands * GROUP, lanes)
    high, low = split(spread)
    r_high, r_low = split(right)
    return dot_nt(
        jnp.concatenate([high, low, high], axis=1),
        jnp.concatenate([r_high, r_high, r_low], axis=1),
    )


def momentum_kernel(momentum_ref, coeffs_ref, left_ref, right_ref, out_ref):
    own = encode(decay_rate * momentum_ref[0], left_ref[...], right_ref[...])
    out_ref[...] = own + jnp.sum(coeffs_ref[...], axis=0)


def plane_coeffs(momentum, coeffs, left, right):
    return pl.pallas_call(
        momentum_kernel,
        out_shape=jax.ShapeDtypeStruct(coeffs.shape[1:], f32),
        in_specs=whole(4),
        out_specs=pl.BlockSpec(memory_space=pltpu.VMEM),
        compiler_params=params(16),
        cost_estimate=COST,
    )(momentum, coeffs, left, right)


def update_kernel(coeffs_ref, left_ref, right_ref, out_ref):
    total = jnp.sum(coeffs_ref[...], axis=0)
    out_ref[...] = decode(total, left_ref[...], right_ref[...]).astype(bf16)


def decoded_update(coeffs, left, right, rows):
    return pl.pallas_call(
        update_kernel,
        out_shape=jax.ShapeDtypeStruct((rows, right.shape[0]), bf16),
        in_specs=whole(3),
        out_specs=pl.BlockSpec(memory_space=pltpu.VMEM),
        compiler_params=params(16),
        cost_estimate=COST,
    )(coeffs, left, right)


def term(ref, side, columns):
    rows = ref.shape[0] - ref.shape[1]
    return dot(ref[0:rows, :], ref[rows:, side * columns : (side + 1) * columns])


def terms(refs, side, columns):
    total = term(refs[0], side, columns)
    for ref in refs[1:]:
        total = total + term(ref, side, columns)
    return total


def other_kernel(*refs):
    *packet_refs, out_ref = refs
    out_ref[...] = terms(packet_refs, 1, out_ref.shape[1])


def other_product(packets):
    length, width = packets[0].shape
    return pl.pallas_call(
        other_kernel,
        out_shape=jax.ShapeDtypeStruct((length - width, width // 2), f32),
        in_specs=whole(len(packets)),
        out_specs=pl.BlockSpec(memory_space=pltpu.VMEM),
        compiler_params=params(16),
        cost_estimate=COST,
    )(*packets)


def fresh_kernel(*refs):
    *packet_refs, momentum_ref, out_ref = refs
    out_ref[...] = decay_rate * momentum_ref[0] + terms(packet_refs, 0, out_ref.shape[1])


def own_fresh(packets, momentum):
    return pl.pallas_call(
        fresh_kernel,
        out_shape=jax.ShapeDtypeStruct(momentum.shape[1:], f32),
        in_specs=whole(len(packets) + 1),
        out_specs=pl.BlockSpec(memory_space=pltpu.VMEM),
        compiler_params=params(16),
        cost_estimate=COST,
    )(*packets, momentum)


def residual_kernel(own_ref, other_ref, left_ref, right_ref, out_ref):
    fresh = own_ref[...] + other_ref[...]
    left, right = left_ref[...], right_ref[...]
    out_ref[0] = fresh - decode(encode(fresh, left, right), left, right)


def residual_of(own, other, left, right):
    return pl.pallas_call(
        residual_kernel,
        out_shape=jax.ShapeDtypeStruct((1,) + own.shape, f32),
        in_specs=whole(4),
        out_specs=pl.BlockSpec(memory_space=pltpu.VMEM),
        compiler_params=params(16),
        cost_estimate=COST,
    )(own, other, left, right)


def spot(y, x, core):
    return ((y % SIDE) * SIDE + x % SIDE) * 2 + core


def shifted(block, step, phase):
    pairs = []
    for y in range(SIDE):
        for x in range(SIDE):
            for core in range(2):
                along_x = core == phase
                to = spot(y, x + step, core) if along_x else spot(y + step, x, core)
                pairs.append((spot(y, x, core), to))
    return lax.ppermute(block, "shard", pairs)


def on_device(hidden_acts, out_grads, momentum, kept):
    tok, rows = hidden_acts.shape
    columns = momentum.shape[2]
    shards = out_grads.shape[1] // columns
    replicas = lax.axis_size("rep")
    me = lax.axis_index("shard").astype(jnp.int32)
    core, mine_x, mine_y = me % 2, me // 2 % SIDE, me // (2 * SIDE)

    place = jnp.stack([core, jnp.where(core == 0, mine_x, mine_y), jnp.where(core == 0, mine_y, mine_x)])
    packets = first_packets(place, hidden_acts, out_grads)
    packets = [packets[0]] + [shifted(p, d, 0) for p, d in zip(packets[1:], OFFSETS[1:])]

    coeffs, left, right = local_coeffs(kept, hidden_acts, out_grads, columns)

    coeffs = lax.all_to_all(coeffs, "shard", split_axis=0, concat_axis=0, tiled=True)
    coeffs, *packets = lax.optimization_barrier((coeffs, *packets))

    packets = second_packets(packets, rows)
    packets = [packets[0]] + [shifted(p, d, 1) for p, d in zip(packets[1:], OFFSETS[1:])]

    coeffs = plane_coeffs(momentum, coeffs, left, right)
    coeffs = lax.all_to_all(
        jnp.broadcast_to(coeffs[None], (replicas,) + coeffs.shape),
        "rep",
        split_axis=0,
        concat_axis=0,
        tiled=True,
    )
    coeffs, *packets = lax.optimization_barrier((coeffs, *packets))
    update = decoded_update(coeffs, left, right, rows)

    other = other_product(packets)
    swap = [(i, i ^ 1) for i in range(shards)]
    other = lax.ppermute(other, "shard", swap)
    own = own_fresh(packets, momentum)
    residual = residual_of(own, other, left, right)
    return (residual, update)


def solution(mesh):
    placed = (P(("rep", "shard"), None), P(("rep", "shard"), None), P("rep", None, "shard"), P())
    return jax.shard_map(
        on_device,
        mesh=mesh,
        in_specs=placed,
        out_specs=(P("rep", None, "shard"), P(None, "shard")),
        check_vma=False,
    )
```

```python
import functools
import math

import jax
import jax.numpy as jnp
import numpy as np
from jax import lax
from jax.experimental import pallas as pl
from jax.experimental.pallas import tpu as pltpu
from jax.sharding import PartitionSpec as P

GROUP = 64
KEPT = 32
SIDE = 4
CHIPS = SIDE * SIDE
OFFSETS = (0, 2, 1, -1)
FAR, NEAR = 1, (0, 2, 3)

decay_rate = 0.9
f32 = jnp.float32
bf16 = jnp.bfloat16
HIGHEST = lax.Precision.HIGHEST
MIB = 1 << 20
COST = pl.CostEstimate(flops=0, bytes_accessed=0, transcendentals=0)


def dot(a, b, precision=None):
    return jnp.dot(a, b, preferred_element_type=f32, precision=precision)


def dot_nt(a, b, precision=None):
    return lax.dot_general(
        a, b, (((1,), (1,)), ((), ())), preferred_element_type=f32, precision=precision
    )


def whole(n):
    return [pl.BlockSpec(memory_space=pltpu.VMEM)] * n


def params(mib=48):
    return pltpu.CompilerParams(vmem_limit_bytes=mib * MIB)


def first_kernel(place_ref, acts_hbm, grads_hbm, *refs):
    *out_refs, acts_ref, grads_ref, sems = refs
    copies = [
        pltpu.make_async_copy(acts_hbm, acts_ref, sems.at[0]),
        pltpu.make_async_copy(grads_hbm, grads_ref, sems.at[1]),
    ]
    for copy in copies:
        copy.start()
    tok, rows = acts_ref.shape
    width = out_refs[0].shape[1]
    depth = rows * tok // width
    half = width // 2
    core, near, far = place_ref[0], place_ref[1], place_ref[2]
    copies[0].wait()
    acts_t = acts_ref[...].astype(f32).T.astype(bf16)
    for q in range(width // tok):
        for ref in out_refs:
            ref[0:depth, q * tok : (q + 1) * tok] = acts_t[q * depth : (q + 1) * depth]
    copies[1].wait()
    for i, ref in enumerate(out_refs):
        a = (near + OFFSETS[i] + SIDE) % SIDE
        for j, d in enumerate(OFFSETS):
            b = (far + d + SIDE) % SIDE
            chip = jnp.where(core == 0, b * SIDE + a, a * SIDE + b)
            for h in range(2):
                start = pl.multiple_of(chip * width + (core + h) % 2 * half, half)
                ref[depth + j * tok : depth + (j + 1) * tok, h * half : (h + 1) * half] = grads_ref[
                    :, pl.ds(start, half)
                ]


def first_packets(place, acts, grads):
    tok, rows = acts.shape
    width = grads.shape[1] // CHIPS
    packet = jax.ShapeDtypeStruct((rows * tok // width + SIDE * tok, width), bf16)
    return pl.pallas_call(
        first_kernel,
        out_shape=(packet,) * SIDE,
        in_specs=[pl.BlockSpec(memory_space=pltpu.SMEM)]
        + [pl.BlockSpec(memory_space=pltpu.HBM)] * 2,
        out_specs=tuple(whole(SIDE)),
        scratch_shapes=[
            pltpu.VMEM(acts.shape, bf16),
            pltpu.VMEM(grads.shape, bf16),
            pltpu.SemaphoreType.DMA((2,)),
        ],
        compiler_params=params(16),
        cost_estimate=COST,
    )(place, *(pltpu.with_memory_space_constraint(a, pltpu.HBM) for a in (acts, grads)))


def second_kernel(*refs):
    in_refs, out_refs = refs[:SIDE], refs[SIDE:]
    length, width = out_refs[0].shape
    tok = width // SIDE
    rows = length - SIDE * tok
    depth = rows * tok // width
    for i, ref in enumerate(in_refs):
        for q in range(SIDE):
            quarter = ref[0:depth, q * tok : (q + 1) * tok]
            for out_ref in out_refs:
                out_ref[q * depth : (q + 1) * depth, i * tok : (i + 1) * tok] = quarter
        for j, out_ref in zip(NEAR, out_refs):
            out_ref[rows + i * tok : rows + (i + 1) * tok, :] = ref[
                depth + j * tok : depth + (j + 1) * tok, :
            ]


def second_packets(packets, rows):
    length, width = packets[0].shape
    packet = jax.ShapeDtypeStruct((rows + width, width), bf16)
    return pl.pallas_call(
        second_kernel,
        out_shape=(packet,) * len(NEAR),
        in_specs=whole(SIDE),
        out_specs=tuple(whole(len(NEAR))),
        compiler_params=params(16),
        cost_estimate=COST,
    )(*packets)


BAND = 128


def partial(refs, j):
    length, width = refs[0].shape
    tok = width // SIDE
    depth = length - SIDE * tok
    grads = jnp.concatenate(
        [ref[depth + j * tok : depth + (j + 1) * tok, :] for ref in refs], axis=0
    )
    blocks = []
    for q in range(SIDE):
        acts = jnp.concatenate([ref[0:depth, q * tok : (q + 1) * tok] for ref in refs], axis=1)
        blocks.append(dot(acts, grads))
    return blocks


def coded_kernel(j, *refs):
    *packet_refs, out_ref = refs
    blocks = partial(packet_refs, j)
    depth, width = blocks[0].shape
    exponents = []
    for q, block in enumerate(blocks):
        for r in range(0, depth, BAND):
            values = block[r : r + BAND]
            largest = jnp.max(jnp.abs(values), axis=0, keepdims=True)
            exponent = jnp.floor(jnp.log2(jnp.maximum(largest, 1e-30))) + 1.0
            scaled = jnp.clip(jnp.round(values * jnp.exp2(15.0 - exponent)), -32767.0, 32767.0)
            start = q * depth + r
            out_ref[start : start + BAND, :] = scaled.astype(jnp.int32).astype(jnp.int16)
            exponents.append(exponent)
    exponents = jnp.concatenate(exponents + [jnp.zeros_like(exponents[0])] * 8, axis=0)
    out_ref[SIDE * depth :, :] = exponents.astype(jnp.int32).astype(jnp.int16)


def coded_partial(packets, j):
    length, width = packets[0].shape
    rows = SIDE * (length - width)
    return pl.pallas_call(
        functools.partial(coded_kernel, j),
        out_shape=jax.ShapeDtypeStruct((rows + 16, width), jnp.int16),
        in_specs=whole(SIDE),
        out_specs=pl.BlockSpec(memory_space=pltpu.VMEM),
        compiler_params=params(16),
        cost_estimate=COST,
    )(*packets)


def decoded(ref, r, lanes):
    rows = ref.shape[0] - 16
    exponent = ref[rows:, lanes].astype(jnp.int32).astype(f32)[r // BAND : r // BAND + 1]
    return ref[r : r + BAND, lanes].astype(jnp.int32).astype(f32) * jnp.exp2(exponent - 15.0)


def split(a):
    high = a.astype(bf16)
    return high, (a - high.astype(f32)).astype(bf16)


def split3(a):
    high = a.astype(bf16)
    rest = a - high.astype(f32)
    middle = rest.astype(bf16)
    return high, middle, (rest - middle.astype(f32)).astype(bf16)


BATCH = 8


def coeff_kernel(kept_ref, table_ref, acts_ref, grads_ref, out_ref, left_ref, right_ref, twice_ref):
    tok, rows = acts_ref.shape
    bands = rows // GROUP
    groups, _, lanes = out_ref.shape
    columns = right_ref.shape[0]

    frequency = lax.broadcasted_iota(jnp.int32, (GROUP, lanes), 0)
    table = table_ref[...]
    kept_lanes = jnp.concatenate([kept_ref[...]] * (lanes // KEPT), axis=1)
    picked_row = jnp.where(frequency == kept_lanes // GROUP, 1.0, 0.0)
    picked_column = jnp.where(frequency == kept_lanes % GROUP, 1.0, 0.0)
    left = dot(table, picked_row, HIGHEST)
    tall = dot(table, picked_column, HIGHEST)
    left_ref[...] = left
    lane = lax.broadcasted_iota(jnp.int32, (GROUP, lanes), 1)
    right = jnp.concatenate(
        [jnp.where(lane // KEPT == b, tall, 0.0) for b in range(columns // GROUP)], axis=0
    )
    right_ref[...] = right
    pieces = jnp.concatenate(split(right), axis=1)

    acts_t = acts_ref[...].astype(f32).T.astype(bf16)
    twice_ref[:, 0:tok] = acts_t
    twice_ref[:, tok : 2 * tok] = acts_t

    def step(i, carry):
        start = pl.multiple_of(i * BATCH * columns, BATCH * columns)
        grads = jnp.concatenate(
            [grads_ref[:, pl.ds(start + j * columns, columns)] for j in range(BATCH)], axis=0
        )
        moved = dot(grads, pieces)
        high, low = split(moved[:, :lanes] + moved[:, lanes:])
        for j in range(0, BATCH, 2):
            both = [jnp.concatenate([p[m * tok : (m + 1) * tok] for p in (high, low)], axis=0) for m in (j, j + 1)]
            product = dot(twice_ref[...], jnp.concatenate(both, axis=1))
            for m in range(2):
                part = product[:, m * lanes : (m + 1) * lanes].reshape(bands, GROUP, lanes) * left[None]
                out_ref[pl.ds(i * BATCH + j + m, 1)] = jnp.sum(part, axis=1)[None]
        return carry

    lax.fori_loop(0, groups // BATCH, step, 0)


def local_coeffs(kept, acts, grads, columns):
    tok, rows = acts.shape
    bands = rows // GROUP
    lanes = columns // GROUP * KEPT
    frequency = np.arange(GROUP, dtype=np.float32)[None, :]
    position = np.arange(GROUP, dtype=np.float32)[:, None]
    table = np.cos(
        np.float32(math.pi) * (2.0 * position + 1.0) * frequency / np.float32(2.0 * GROUP)
    ) * np.float32(math.sqrt(2.0 / GROUP))
    table = (table * np.where(frequency == 0.0, math.sqrt(0.5), 1.0)).astype(np.float32)
    return pl.pallas_call(
        coeff_kernel,
        out_shape=(
            jax.ShapeDtypeStruct((grads.shape[1] // columns, bands, lanes), f32),
            jax.ShapeDtypeStruct((GROUP, lanes), f32),
            jax.ShapeDtypeStruct((columns, lanes), f32),
        ),
        in_specs=whole(4),
        out_specs=tuple(whole(3)),
        scratch_shapes=[pltpu.VMEM((rows, 2 * tok), bf16)],
        compiler_params=params(16),
        cost_estimate=COST,
    )(kept[None, :], jnp.asarray(table), acts, grads)


def encode(field, left, right):
    rows = field.shape[0]
    high, low = split(field)
    r_high, r_low = split(right)
    moved = dot(high, r_high) + dot(low, r_high) + dot(high, r_low)
    moved = moved.reshape(rows // GROUP, GROUP, right.shape[1]) * left[None]
    return jnp.sum(moved, axis=1)


def decode(coeffs, left, right):
    bands, lanes = coeffs.shape
    spread = (coeffs[:, None, :] * left[None]).reshape(bands * GROUP, lanes)
    high, low = split(spread)
    r_high, r_low = split(right)
    return dot_nt(
        jnp.concatenate([high, low, high], axis=1),
        jnp.concatenate([r_high, r_high, r_low], axis=1),
    )


def momentum_kernel(momentum_ref, coeffs_ref, left_ref, right_ref, out_ref):
    own = encode(decay_rate * momentum_ref[0], left_ref[...], right_ref[...])
    out_ref[...] = own + jnp.sum(coeffs_ref[...], axis=0)


def plane_coeffs(momentum, coeffs, left, right):
    return pl.pallas_call(
        momentum_kernel,
        out_shape=jax.ShapeDtypeStruct(coeffs.shape[1:], f32),
        in_specs=whole(4),
        out_specs=pl.BlockSpec(memory_space=pltpu.VMEM),
        compiler_params=params(16),
        cost_estimate=COST,
    )(momentum, coeffs, left, right)


def update_kernel(coeffs_ref, left_ref, right_ref, out_ref):
    total = jnp.sum(coeffs_ref[...], axis=0)
    out_ref[...] = decode(total, left_ref[...], right_ref[...]).astype(bf16)


def decoded_update(coeffs, left, right, rows):
    return pl.pallas_call(
        update_kernel,
        out_shape=jax.ShapeDtypeStruct((rows, right.shape[0]), bf16),
        in_specs=whole(3),
        out_specs=pl.BlockSpec(memory_space=pltpu.VMEM),
        compiler_params=params(16),
        cost_estimate=COST,
    )(coeffs, left, right)


def half_gradient(packet_refs, coded_ref, side, columns):
    lanes = slice(side * columns, (side + 1) * columns)
    total = None
    for ref in packet_refs:
        rows = ref.shape[0] - ref.shape[1]
        term = dot(ref[0:rows, :], ref[rows:, lanes])
        total = term if total is None else total + term
    for r in range(0, total.shape[0], BAND):
        yield r, total[r : r + BAND] + decoded(coded_ref, r, lanes)


def other_kernel(*refs):
    *packet_refs, coded_ref, out_ref = refs
    for r, total in half_gradient(packet_refs, coded_ref, 1, out_ref.shape[1]):
        out_ref[r : r + BAND, :] = total


def other_half(packets, coded):
    length, width = packets[0].shape
    return pl.pallas_call(
        other_kernel,
        out_shape=jax.ShapeDtypeStruct((length - width, width // 2), f32),
        in_specs=whole(len(packets) + 1),
        out_specs=pl.BlockSpec(memory_space=pltpu.VMEM),
        compiler_params=params(16),
        cost_estimate=COST,
    )(*packets, coded)


def fresh_kernel(*refs):
    *packet_refs, coded_ref, momentum_ref, out_ref = refs
    for r, total in half_gradient(packet_refs, coded_ref, 0, out_ref.shape[1]):
        out_ref[r : r + BAND, :] = decay_rate * momentum_ref[0, r : r + BAND, :] + total


def own_fresh(packets, coded, momentum):
    return pl.pallas_call(
        fresh_kernel,
        out_shape=jax.ShapeDtypeStruct(momentum.shape[1:], f32),
        in_specs=whole(len(packets) + 2),
        out_specs=pl.BlockSpec(memory_space=pltpu.VMEM),
        compiler_params=params(16),
        cost_estimate=COST,
    )(*packets, coded, momentum)


def residual_kernel(own_ref, other_ref, left_ref, right_ref, out_ref):
    fresh = own_ref[...] + other_ref[...]
    left, right = left_ref[...], right_ref[...]
    out_ref[0] = fresh - decode(encode(fresh, left, right), left, right)


def residual_of(own, other, left, right):
    return pl.pallas_call(
        residual_kernel,
        out_shape=jax.ShapeDtypeStruct((1,) + own.shape, f32),
        in_specs=whole(4),
        out_specs=pl.BlockSpec(memory_space=pltpu.VMEM),
        compiler_params=params(16),
        cost_estimate=COST,
    )(own, other, left, right)


def spot(y, x, core):
    return ((y % SIDE) * SIDE + x % SIDE) * 2 + core


def shifted(block, step, phase):
    pairs = []
    for y in range(SIDE):
        for x in range(SIDE):
            for core in range(2):
                along_x = core == phase
                to = spot(y, x + step, core) if along_x else spot(y + step, x, core)
                pairs.append((spot(y, x, core), to))
    return lax.ppermute(block, "shard", pairs)


def on_device(hidden_acts, out_grads, momentum, kept):
    tok, rows = hidden_acts.shape
    columns = momentum.shape[2]
    shards = out_grads.shape[1] // columns
    replicas = lax.axis_size("rep")
    me = lax.axis_index("shard").astype(jnp.int32)
    core, mine_x, mine_y = me % 2, me // 2 % SIDE, me // (2 * SIDE)

    place = jnp.stack([core, jnp.where(core == 0, mine_x, mine_y), jnp.where(core == 0, mine_y, mine_x)])
    packets = first_packets(place, hidden_acts, out_grads)
    packets = [packets[0]] + [shifted(p, d, 0) for p, d in zip(packets[1:], OFFSETS[1:])]

    coeffs, left, right = local_coeffs(kept, hidden_acts, out_grads, columns)

    coeffs = lax.all_to_all(coeffs, "shard", split_axis=0, concat_axis=0, tiled=True)
    coeffs, *packets = lax.optimization_barrier((coeffs, *packets))

    coded = shifted(coded_partial(packets, FAR), OFFSETS[FAR], 1)
    packets = second_packets(packets, rows)
    packets = [packets[0]] + [shifted(p, OFFSETS[j], 1) for p, j in zip(packets[1:], NEAR[1:])]

    coeffs = plane_coeffs(momentum, coeffs, left, right)
    coeffs = lax.all_to_all(
        jnp.broadcast_to(coeffs[None], (replicas,) + coeffs.shape),
        "rep",
        split_axis=0,
        concat_axis=0,
        tiled=True,
    )
    coeffs, coded, *packets = lax.optimization_barrier((coeffs, coded, *packets))
    update = decoded_update(coeffs, left, right, rows)

    other = other_half(packets, coded)
    swap = [(i, i ^ 1) for i in range(shards)]
    other = lax.ppermute(other, "shard", swap)
    own = own_fresh(packets, coded, momentum)
    residual = residual_of(own, other, left, right)
    return (residual, update)


def solution(mesh):
    placed = (P(("rep", "shard"), None), P(("rep", "shard"), None), P("rep", None, "shard"), P())
    return jax.shard_map(
        on_device,
        mesh=mesh,
        in_specs=placed,
        out_specs=(P("rep", None, "shard"), P(None, "shard")),
        check_vma=False,
    )
```

```python
import functools
import math

import jax
import jax.numpy as jnp
import numpy as np
from jax import lax
from jax.experimental import pallas as pl
from jax.experimental.pallas import tpu as pltpu
from jax.sharding import PartitionSpec as P

GROUP = 64
KEPT = 32
SIDE = 4
CHIPS = SIDE * SIDE
OFFSETS = (0, 2, 1, -1)
FAR, NEAR = 1, (0, 2, 3)

decay_rate = 0.9
f32 = jnp.float32
bf16 = jnp.bfloat16
HIGHEST = lax.Precision.HIGHEST
MIB = 1 << 20
COST = pl.CostEstimate(flops=0, bytes_accessed=0, transcendentals=0)


def dot(a, b, precision=None):
    return jnp.dot(a, b, preferred_element_type=f32, precision=precision)


def dot_nt(a, b, precision=None):
    return lax.dot_general(
        a, b, (((1,), (1,)), ((), ())), preferred_element_type=f32, precision=precision
    )


def whole(n):
    return [pl.BlockSpec(memory_space=pltpu.VMEM)] * n


def params(mib=48):
    return pltpu.CompilerParams(vmem_limit_bytes=mib * MIB)


def first_kernel(me_ref, acts_hbm, grads_hbm, table_hbm, *refs):
    *out_refs, acts_ref, grads_ref, table_ref, sems = refs
    copies = [
        pltpu.make_async_copy(acts_hbm, acts_ref, sems.at[0]),
        pltpu.make_async_copy(grads_hbm, grads_ref, sems.at[1]),
        pltpu.make_async_copy(table_hbm, table_ref, sems.at[2]),
    ]
    for copy in copies:
        copy.start()
    tok, rows = acts_ref.shape
    width = out_refs[0].shape[1]
    depth = rows * tok // width
    half = width // 2
    me = me_ref[0]
    core, x, y = me % 2, me // 2 % SIDE, me // (2 * SIDE)
    near, far = jnp.where(core == 0, x, y), jnp.where(core == 0, y, x)
    copies[0].wait()
    acts_t = acts_ref[...].astype(f32).T.astype(bf16)
    for q in range(width // tok):
        for ref in out_refs:
            ref[0:depth, q * tok : (q + 1) * tok] = acts_t[q * depth : (q + 1) * depth]
    copies[1].wait()
    copies[2].wait()
    for i, ref in enumerate(out_refs):
        a = (near + OFFSETS[i] + SIDE) % SIDE
        for j, d in enumerate(OFFSETS):
            b = (far + d + SIDE) % SIDE
            chip = jnp.where(core == 0, b * SIDE + a, a * SIDE + b)
            for h in range(2):
                start = pl.multiple_of(chip * width + (core + h) % 2 * half, half)
                ref[depth + j * tok : depth + (j + 1) * tok, h * half : (h + 1) * half] = grads_ref[
                    :, pl.ds(start, half)
                ]


def first_packets(me, *inputs):
    tok, rows = inputs[0].shape
    width = inputs[1].shape[1] // CHIPS
    packet = jax.ShapeDtypeStruct((rows * tok // width + SIDE * tok, width), bf16)
    held = tuple(jax.ShapeDtypeStruct(a.shape, a.dtype) for a in inputs)
    *packets, acts, grads, table = pl.pallas_call(
        first_kernel,
        out_shape=(packet,) * SIDE + held,
        in_specs=[pl.BlockSpec(memory_space=pltpu.SMEM)]
        + [pl.BlockSpec(memory_space=pltpu.HBM)] * len(inputs),
        out_specs=tuple(whole(SIDE + len(inputs))),
        scratch_shapes=[pltpu.SemaphoreType.DMA((len(inputs),))],
        compiler_params=params(16),
        cost_estimate=COST,
    )(me[None], *(pltpu.with_memory_space_constraint(a, pltpu.HBM) for a in inputs))
    return packets, acts, grads, table


def second_kernel(*refs):
    in_refs, out_refs = refs[:SIDE], refs[SIDE:]
    length, width = out_refs[0].shape
    tok = width // SIDE
    rows = length - SIDE * tok
    depth = rows * tok // width
    for i, ref in enumerate(in_refs):
        for q in range(SIDE):
            quarter = ref[0:depth, q * tok : (q + 1) * tok]
            for out_ref in out_refs:
                out_ref[q * depth : (q + 1) * depth, i * tok : (i + 1) * tok] = quarter
        for j, out_ref in zip(NEAR, out_refs):
            out_ref[rows + i * tok : rows + (i + 1) * tok, :] = ref[
                depth + j * tok : depth + (j + 1) * tok, :
            ]


def second_packets(packets, rows):
    length, width = packets[0].shape
    packet = jax.ShapeDtypeStruct((rows + width, width), bf16)
    return pl.pallas_call(
        second_kernel,
        out_shape=(packet,) * len(NEAR),
        in_specs=whole(SIDE),
        out_specs=tuple(whole(len(NEAR))),
        compiler_params=params(16),
        cost_estimate=COST,
    )(*packets)


BAND = 128


def partial(refs, j):
    length, width = refs[0].shape
    tok = width // SIDE
    depth = length - SIDE * tok
    grads = jnp.concatenate(
        [ref[depth + j * tok : depth + (j + 1) * tok, :] for ref in refs], axis=0
    )
    blocks = []
    for q in range(SIDE):
        acts = jnp.concatenate([ref[0:depth, q * tok : (q + 1) * tok] for ref in refs], axis=1)
        blocks.append(dot(acts, grads))
    return blocks


def coded_kernel(j, *refs):
    *packet_refs, out_ref = refs
    blocks = partial(packet_refs, j)
    depth, width = blocks[0].shape
    exponents = []
    for q, block in enumerate(blocks):
        for r in range(0, depth, BAND):
            values = block[r : r + BAND]
            largest = jnp.max(jnp.abs(values), axis=0, keepdims=True)
            exponent = jnp.floor(jnp.log2(jnp.maximum(largest, 1e-30))) + 1.0
            scaled = jnp.clip(jnp.round(values * jnp.exp2(15.0 - exponent)), -32767.0, 32767.0)
            start = q * depth + r
            out_ref[start : start + BAND, :] = scaled.astype(jnp.int32).astype(jnp.int16)
            exponents.append(exponent)
    exponents = jnp.concatenate(exponents + [jnp.zeros_like(exponents[0])] * 8, axis=0)
    out_ref[SIDE * depth :, :] = exponents.astype(jnp.int32).astype(jnp.int16)


def coded_partial(packets, j):
    length, width = packets[0].shape
    rows = SIDE * (length - width)
    return pl.pallas_call(
        functools.partial(coded_kernel, j),
        out_shape=jax.ShapeDtypeStruct((rows + 16, width), jnp.int16),
        in_specs=whole(SIDE),
        out_specs=pl.BlockSpec(memory_space=pltpu.VMEM),
        compiler_params=params(16),
        cost_estimate=COST,
    )(*packets)


def decoded(ref, r, lanes):
    rows = ref.shape[0] - 16
    exponent = ref[rows:, lanes].astype(jnp.int32).astype(f32)[r // BAND : r // BAND + 1]
    return ref[r : r + BAND, lanes].astype(jnp.int32).astype(f32) * jnp.exp2(exponent - 15.0)


def split(a):
    high = a.astype(bf16)
    return high, (a - high.astype(f32)).astype(bf16)


def split3(a):
    high = a.astype(bf16)
    rest = a - high.astype(f32)
    middle = rest.astype(bf16)
    return high, middle, (rest - middle.astype(f32)).astype(bf16)


BATCH = 8


def coeff_kernel(kept_ref, table_ref, acts_ref, grads_ref, out_ref, left_ref, right_ref, twice_ref):
    tok, rows = acts_ref.shape
    bands = rows // GROUP
    groups, _, lanes = out_ref.shape
    columns = right_ref.shape[0]

    frequency = lax.broadcasted_iota(jnp.int32, (GROUP, lanes), 0)
    table = table_ref[...]
    kept_lanes = jnp.concatenate([kept_ref[...]] * (lanes // KEPT), axis=1)
    picked_row = jnp.where(frequency == kept_lanes // GROUP, 1.0, 0.0)
    picked_column = jnp.where(frequency == kept_lanes % GROUP, 1.0, 0.0)
    left = dot(table, picked_row, HIGHEST)
    tall = dot(table, picked_column, HIGHEST)
    left_ref[...] = left
    lane = lax.broadcasted_iota(jnp.int32, (GROUP, lanes), 1)
    right = jnp.concatenate(
        [jnp.where(lane // KEPT == b, tall, 0.0) for b in range(columns // GROUP)], axis=0
    )
    right_ref[...] = right
    pieces = jnp.concatenate(split(right), axis=1)

    acts_t = acts_ref[...].astype(f32).T.astype(bf16)
    twice_ref[:, 0:tok] = acts_t
    twice_ref[:, tok : 2 * tok] = acts_t

    def step(i, carry):
        start = pl.multiple_of(i * BATCH * columns, BATCH * columns)
        grads = jnp.concatenate(
            [grads_ref[:, pl.ds(start + j * columns, columns)] for j in range(BATCH)], axis=0
        )
        moved = dot(grads, pieces)
        high, low = split(moved[:, :lanes] + moved[:, lanes:])
        for j in range(0, BATCH, 2):
            both = [jnp.concatenate([p[m * tok : (m + 1) * tok] for p in (high, low)], axis=0) for m in (j, j + 1)]
            product = dot(twice_ref[...], jnp.concatenate(both, axis=1))
            for m in range(2):
                part = product[:, m * lanes : (m + 1) * lanes].reshape(bands, GROUP, lanes) * left[None]
                out_ref[pl.ds(i * BATCH + j + m, 1)] = jnp.sum(part, axis=1)[None]
        return carry

    lax.fori_loop(0, groups // BATCH, step, 0, unroll=groups // BATCH)


def cosine_table():
    frequency = np.arange(GROUP, dtype=np.float32)[None, :]
    position = np.arange(GROUP, dtype=np.float32)[:, None]
    table = np.cos(
        np.float32(math.pi) * (2.0 * position + 1.0) * frequency / np.float32(2.0 * GROUP)
    ) * np.float32(math.sqrt(2.0 / GROUP))
    table = (table * np.where(frequency == 0.0, math.sqrt(0.5), 1.0)).astype(np.float32)
    return jnp.asarray(table)


def local_coeffs(kept, table, acts, grads, columns):
    tok, rows = acts.shape
    bands = rows // GROUP
    lanes = columns // GROUP * KEPT
    return pl.pallas_call(
        coeff_kernel,
        out_shape=(
            jax.ShapeDtypeStruct((grads.shape[1] // columns, bands, lanes), f32),
            jax.ShapeDtypeStruct((GROUP, lanes), f32),
            jax.ShapeDtypeStruct((columns, lanes), f32),
        ),
        in_specs=whole(4),
        out_specs=tuple(whole(3)),
        scratch_shapes=[pltpu.VMEM((rows, 2 * tok), bf16)],
        compiler_params=params(16),
        cost_estimate=COST,
    )(kept[None, :], table, acts, grads)


def encode(field, left, right):
    rows = field.shape[0]
    high, low = split(field)
    r_high, r_low = split(right)
    lanes = right.shape[1]
    moved = dot(high, jnp.concatenate([r_high, r_low], axis=1))
    moved = moved[:, :lanes] + (moved[:, lanes:] + dot(low, r_high))
    moved = moved.reshape(rows // GROUP, GROUP, right.shape[1]) * left[None]
    return jnp.sum(moved, axis=1)


def decode(coeffs, left, right):
    bands, lanes = coeffs.shape
    spread = (coeffs[:, None, :] * left[None]).reshape(bands * GROUP, lanes)
    high, low = split(spread)
    r_high, r_low = split(right)
    return dot_nt(
        jnp.concatenate([high, low, high], axis=1),
        jnp.concatenate([r_high, r_high, r_low], axis=1),
    )


def momentum_kernel(momentum_ref, coeffs_ref, left_ref, right_ref, out_ref):
    own = encode(decay_rate * momentum_ref[0], left_ref[...], right_ref[...])
    out_ref[...] = own + jnp.sum(coeffs_ref[...], axis=0)


def plane_coeffs(momentum, coeffs, left, right):
    return pl.pallas_call(
        momentum_kernel,
        out_shape=jax.ShapeDtypeStruct(coeffs.shape[1:], f32),
        in_specs=whole(4),
        out_specs=pl.BlockSpec(memory_space=pltpu.VMEM),
        compiler_params=params(16),
        cost_estimate=COST,
    )(momentum, coeffs, left, right)


def update_kernel(coeffs_ref, left_ref, right_ref, out_ref):
    total = jnp.sum(coeffs_ref[...], axis=0)
    out_ref[...] = decode(total, left_ref[...], right_ref[...]).astype(bf16)


def decoded_update(coeffs, left, right, rows):
    return pl.pallas_call(
        update_kernel,
        out_shape=jax.ShapeDtypeStruct((rows, right.shape[0]), bf16),
        in_specs=whole(3),
        out_specs=pl.BlockSpec(memory_space=pltpu.VMEM),
        compiler_params=params(16),
        cost_estimate=COST,
    )(coeffs, left, right)


def half_gradient(packet_refs, coded_ref, side, columns):
    lanes = slice(side * columns, (side + 1) * columns)
    total = None
    for ref in packet_refs:
        rows = ref.shape[0] - ref.shape[1]
        term = dot(ref[0:rows, :], ref[rows:, lanes])
        total = term if total is None else total + term
    for r in range(0, total.shape[0], BAND):
        yield r, total[r : r + BAND] + decoded(coded_ref, r, lanes)


def other_kernel(*refs):
    *packet_refs, coded_ref, out_ref = refs
    for r, total in half_gradient(packet_refs, coded_ref, 1, out_ref.shape[1]):
        out_ref[r : r + BAND, :] = total


def other_half(packets, coded):
    length, width = packets[0].shape
    return pl.pallas_call(
        other_kernel,
        out_shape=jax.ShapeDtypeStruct((length - width, width // 2), f32),
        in_specs=whole(len(packets) + 1),
        out_specs=pl.BlockSpec(memory_space=pltpu.VMEM),
        compiler_params=params(16),
        cost_estimate=COST,
    )(*packets, coded)


def fresh_kernel(*refs):
    *packet_refs, coded_ref, momentum_ref, out_ref = refs
    for r, total in half_gradient(packet_refs, coded_ref, 0, out_ref.shape[1]):
        out_ref[r : r + BAND, :] = decay_rate * momentum_ref[0, r : r + BAND, :] + total


def own_fresh(packets, coded, momentum):
    return pl.pallas_call(
        fresh_kernel,
        out_shape=jax.ShapeDtypeStruct(momentum.shape[1:], f32),
        in_specs=whole(len(packets) + 2),
        out_specs=pl.BlockSpec(memory_space=pltpu.VMEM),
        compiler_params=params(16),
        cost_estimate=COST,
    )(*packets, coded, momentum)


def residual_kernel(own_ref, other_ref, left_ref, right_ref, out_ref):
    fresh = own_ref[...] + other_ref[...]
    left, right = left_ref[...], right_ref[...]
    out_ref[0] = fresh - decode(encode(fresh, left, right), left, right)


def residual_of(own, other, left, right):
    return pl.pallas_call(
        residual_kernel,
        out_shape=jax.ShapeDtypeStruct((1,) + own.shape, f32),
        in_specs=whole(4),
        out_specs=pl.BlockSpec(memory_space=pltpu.VMEM),
        compiler_params=params(16),
        cost_estimate=COST,
    )(own, other, left, right)


def spot(y, x, core):
    return ((y % SIDE) * SIDE + x % SIDE) * 2 + core


def shifted(block, step, phase):
    pairs = []
    for y in range(SIDE):
        for x in range(SIDE):
            for core in range(2):
                along_x = core == phase
                to = spot(y, x + step, core) if along_x else spot(y + step, x, core)
                pairs.append((spot(y, x, core), to))
    return lax.ppermute(block, "shard", pairs)


def on_device(hidden_acts, out_grads, momentum, kept):
    tok, rows = hidden_acts.shape
    columns = momentum.shape[2]
    shards = out_grads.shape[1] // columns
    replicas = lax.axis_size("rep")
    me = lax.axis_index("shard").astype(jnp.int32)

    packets, acts, grads, table = first_packets(me, hidden_acts, out_grads, cosine_table())
    packets = [packets[0]] + [shifted(p, d, 0) for p, d in zip(packets[1:], OFFSETS[1:])]

    coeffs, left, right = local_coeffs(kept, table, acts, grads, columns)

    coeffs = lax.all_to_all(coeffs, "shard", split_axis=0, concat_axis=0, tiled=True)
    coeffs, *packets = lax.optimization_barrier((coeffs, *packets))

    coded = shifted(coded_partial(packets, FAR), OFFSETS[FAR], 1)
    packets = second_packets(packets, rows)
    packets = [packets[0]] + [shifted(p, OFFSETS[j], 1) for p, j in zip(packets[1:], NEAR[1:])]

    coeffs = plane_coeffs(momentum, coeffs, left, right)
    coeffs = lax.all_to_all(
        jnp.broadcast_to(coeffs[None], (replicas,) + coeffs.shape),
        "rep",
        split_axis=0,
        concat_axis=0,
        tiled=True,
    )
    coeffs, coded, *packets = lax.optimization_barrier((coeffs, coded, *packets))
    update = decoded_update(coeffs, left, right, rows)

    other = other_half(packets, coded)
    swap = [(i, i ^ 1) for i in range(shards)]
    other = lax.ppermute(other, "shard", swap)
    own = own_fresh(packets, coded, momentum)
    residual = residual_of(own, other, left, right)
    return (residual, update)


def solution(mesh):
    placed = (P(("rep", "shard"), None), P(("rep", "shard"), None), P("rep", None, "shard"), P())
    return jax.shard_map(
        on_device,
        mesh=mesh,
        in_specs=placed,
        out_specs=(P("rep", None, "shard"), P(None, "shard")),
        check_vma=False,
    )
```

```python
import functools
import math

import jax
import jax.numpy as jnp
import numpy as np
from jax import lax
from jax.experimental import pallas as pl
from jax.experimental.pallas import tpu as pltpu
from jax.sharding import PartitionSpec as P

GROUP = 64
KEPT = 32
SIDE = 4
CHIPS = SIDE * SIDE
OFFSETS = (0, 2, 1, -1)
FAR, NEAR = 1, (0, 2, 3)

decay_rate = 0.9
f32 = jnp.float32
bf16 = jnp.bfloat16
HIGHEST = lax.Precision.HIGHEST
MIB = 1 << 20
COST = pl.CostEstimate(flops=0, bytes_accessed=0, transcendentals=0)


def dot(a, b, precision=None):
    return jnp.dot(a, b, preferred_element_type=f32, precision=precision)


def dot_nt(a, b, precision=None):
    return lax.dot_general(
        a, b, (((1,), (1,)), ((), ())), preferred_element_type=f32, precision=precision
    )


def whole(n):
    return [pl.BlockSpec(memory_space=pltpu.VMEM)] * n


def params(mib=48):
    return pltpu.CompilerParams(vmem_limit_bytes=mib * MIB)


def place_of(me):
    core, x, y = me % 2, me // 2 % SIDE, me // (2 * SIDE)
    return core, jnp.where(core == 0, x, y), jnp.where(core == 0, y, x)


def gradient_parts(me, i, width):
    core, near, far = place_of(me)
    a = (near + OFFSETS[i] + SIDE) % SIDE
    for j, d in enumerate(OFFSETS):
        b = (far + d + SIDE) % SIDE
        chip = jnp.where(core == 0, b * SIDE + a, a * SIDE + b)
        for h in range(2):
            yield j, h, pl.multiple_of(chip * width + (core + h) % 2 * (width // 2), width // 2)


def far_kernel(me_ref, acts_hbm, grads_hbm, out_ref, acts_ref, sem, sems):
    tok, rows = acts_ref.shape
    width = out_ref.shape[1]
    depth = rows * tok // width
    half = width // 2
    copies = [pltpu.make_async_copy(acts_hbm, acts_ref, sem)]
    for j, h, start in gradient_parts(me_ref[0], FAR, width):
        copies.append(
            pltpu.make_async_copy(
                grads_hbm.at[:, pl.ds(start, half)],
                out_ref.at[depth + j * tok : depth + (j + 1) * tok, h * half : (h + 1) * half],
                sems.at[len(copies) - 1],
            )
        )
    for copy in copies:
        copy.start()
    copies[0].wait()
    acts_t = acts_ref[...].astype(f32).T.astype(bf16)
    for q in range(width // tok):
        out_ref[0:depth, q * tok : (q + 1) * tok] = acts_t[q * depth : (q + 1) * depth]
    for copy in copies[1:]:
        copy.wait()


def near_kernel(me_ref, far_ref, grads_ref, *out_refs):
    tok = grads_ref.shape[0]
    length, width = far_ref.shape
    depth = length - SIDE * tok
    half = width // 2
    for i, ref in zip(NEAR, out_refs):
        ref[0:depth, :] = far_ref[0:depth, :]
        for j, h, start in gradient_parts(me_ref[0], i, width):
            ref[depth + j * tok : depth + (j + 1) * tok, h * half : (h + 1) * half] = grads_ref[
                :, pl.ds(start, half)
            ]


def first_packets(me, acts, grads):
    tok, rows = acts.shape
    width = grads.shape[1] // CHIPS
    packet = jax.ShapeDtypeStruct((rows * tok // width + SIDE * tok, width), bf16)
    far, held = pl.pallas_call(
        far_kernel,
        out_shape=(packet, jax.ShapeDtypeStruct(acts.shape, acts.dtype)),
        in_specs=[pl.BlockSpec(memory_space=pltpu.SMEM)]
        + [pl.BlockSpec(memory_space=pltpu.HBM)] * 2,
        out_specs=tuple(whole(2)),
        scratch_shapes=[pltpu.SemaphoreType.DMA, pltpu.SemaphoreType.DMA((2 * SIDE,))],
        compiler_params=params(16),
        cost_estimate=COST,
    )(me[None], *(pltpu.with_memory_space_constraint(a, pltpu.HBM) for a in (acts, grads)))
    near = pl.pallas_call(
        near_kernel,
        out_shape=(packet,) * len(NEAR),
        in_specs=[pl.BlockSpec(memory_space=pltpu.SMEM)] + whole(2),
        out_specs=tuple(whole(len(NEAR))),
        compiler_params=params(16),
        cost_estimate=COST,
    )(me[None], far, grads)
    return [near[0], far, near[1], near[2]], held


BAND = 128


def partial(refs, j, lanes=slice(None)):
    length, width = refs[0].shape
    tok = width // SIDE
    depth = length - SIDE * tok
    grads = jnp.concatenate(
        [ref[depth + j * tok : depth + (j + 1) * tok, lanes] for ref in refs], axis=0
    )
    blocks = []
    for q in range(SIDE):
        acts = jnp.concatenate([ref[0:depth, q * tok : (q + 1) * tok] for ref in refs], axis=1)
        blocks.append(dot(acts, grads))
    return blocks


MARGIN = 0.998


def coded_kernel(chips, *refs):
    packet_refs, out_refs = refs[:SIDE], refs[SIDE:]
    for j, out_ref in zip(chips, out_refs):
        blocks = partial(packet_refs, j)
        depth = blocks[0].shape[0]
        exponents = []
        for q, block in enumerate(blocks):
            for r in range(0, depth, BAND):
                values = block[r : r + BAND]
                largest = jnp.max(jnp.abs(values), axis=0, keepdims=True)
                exponent = jnp.floor(jnp.log2(jnp.maximum(largest, 1e-30))) + 1.0
                scaled = jnp.round(values * (MARGIN * jnp.exp2(15.0 - exponent)))
                start = q * depth + r
                out_ref[start : start + BAND, :] = scaled.astype(jnp.int32).astype(jnp.int16)
                exponents.append(exponent)
        exponents = jnp.concatenate(exponents + [jnp.zeros_like(exponents[0])] * 8, axis=0)
        out_ref[SIDE * depth :, :] = exponents.astype(jnp.int32).astype(jnp.int16)


def coded_partials(packets, chips):
    length, width = packets[0].shape
    rows = SIDE * (length - width)
    return pl.pallas_call(
        functools.partial(coded_kernel, chips),
        out_shape=(jax.ShapeDtypeStruct((rows + 16, width), jnp.int16),) * len(chips),
        in_specs=whole(SIDE),
        out_specs=tuple(whole(len(chips))),
        compiler_params=params(16),
        cost_estimate=COST,
    )(*packets)


def decoded(ref, r, lanes):
    rows = ref.shape[0] - 16
    exponent = ref[rows:, lanes].astype(jnp.int32).astype(f32)[r // BAND : r // BAND + 1]
    return ref[r : r + BAND, lanes].astype(jnp.int32).astype(f32) * (jnp.exp2(exponent - 15.0) / MARGIN)


def split(a):
    high = a.astype(bf16)
    return high, (a - high.astype(f32)).astype(bf16)


def split3(a):
    high = a.astype(bf16)
    rest = a - high.astype(f32)
    middle = rest.astype(bf16)
    return high, middle, (rest - middle.astype(f32)).astype(bf16)


BATCH = 8


def coeff_kernel(kept_ref, table_ref, acts_ref, grads_ref, out_ref, left_ref, right_ref, twice_ref):
    tok, rows = acts_ref.shape
    bands = rows // GROUP
    groups, _, lanes = out_ref.shape
    columns = right_ref.shape[0]

    frequency = lax.broadcasted_iota(jnp.int32, (GROUP, lanes), 0)
    table = table_ref[...]
    kept_lanes = jnp.concatenate([kept_ref[...]] * (lanes // KEPT), axis=1)
    picked_row = jnp.where(frequency == kept_lanes // GROUP, 1.0, 0.0)
    picked_column = jnp.where(frequency == kept_lanes % GROUP, 1.0, 0.0)
    left = dot(table, picked_row, HIGHEST)
    tall = dot(table, picked_column, HIGHEST)
    left_ref[...] = left
    lane = lax.broadcasted_iota(jnp.int32, (GROUP, lanes), 1)
    right = jnp.concatenate(
        [jnp.where(lane // KEPT == b, tall, 0.0) for b in range(columns // GROUP)], axis=0
    )
    right_ref[...] = right
    pieces = jnp.concatenate(split(right), axis=1)

    acts_t = acts_ref[...].astype(f32).T.astype(bf16)
    twice_ref[:, 0:tok] = acts_t
    twice_ref[:, tok : 2 * tok] = acts_t

    def step(i, carry):
        start = pl.multiple_of(i * BATCH * columns, BATCH * columns)
        grads = jnp.concatenate(
            [grads_ref[:, pl.ds(start + j * columns, columns)] for j in range(BATCH)], axis=0
        )
        moved = dot(grads, pieces)
        high, low = split(moved[:, :lanes] + moved[:, lanes:])
        for j in range(0, BATCH, 2):
            both = [jnp.concatenate([p[m * tok : (m + 1) * tok] for p in (high, low)], axis=0) for m in (j, j + 1)]
            product = dot(twice_ref[...], jnp.concatenate(both, axis=1))
            for m in range(2):
                part = product[:, m * lanes : (m + 1) * lanes].reshape(bands, GROUP, lanes) * left[None]
                out_ref[pl.ds(i * BATCH + j + m, 1)] = jnp.sum(part, axis=1)[None]
        return carry

    lax.fori_loop(0, groups // BATCH, step, 0, unroll=groups // BATCH)


def cosine_table():
    frequency = np.arange(GROUP, dtype=np.float32)[None, :]
    position = np.arange(GROUP, dtype=np.float32)[:, None]
    table = np.cos(
        np.float32(math.pi) * (2.0 * position + 1.0) * frequency / np.float32(2.0 * GROUP)
    ) * np.float32(math.sqrt(2.0 / GROUP))
    table = (table * np.where(frequency == 0.0, math.sqrt(0.5), 1.0)).astype(np.float32)
    return jnp.asarray(table)


def local_coeffs(kept, table, acts, grads, columns):
    tok, rows = acts.shape
    bands = rows // GROUP
    lanes = columns // GROUP * KEPT
    return pl.pallas_call(
        coeff_kernel,
        out_shape=(
            jax.ShapeDtypeStruct((grads.shape[1] // columns, bands, lanes), f32),
            jax.ShapeDtypeStruct((GROUP, lanes), f32),
            jax.ShapeDtypeStruct((columns, lanes), f32),
        ),
        in_specs=whole(4),
        out_specs=tuple(whole(3)),
        scratch_shapes=[pltpu.VMEM((rows, 2 * tok), bf16)],
        compiler_params=params(16),
        cost_estimate=COST,
    )(kept[None, :], table, acts, grads)


def encode(field, left, right):
    rows = field.shape[0]
    high, low = split(field)
    r_high, r_low = split(right)
    lanes = right.shape[1]
    moved = dot(high, jnp.concatenate([r_high, r_low], axis=1))
    moved = moved[:, :lanes] + (moved[:, lanes:] + dot(low, r_high))
    moved = moved.reshape(rows // GROUP, GROUP, right.shape[1]) * left[None]
    return jnp.sum(moved, axis=1)


def decode(coeffs, left, right):
    bands, lanes = coeffs.shape
    spread = (coeffs[:, None, :] * left[None]).reshape(bands * GROUP, lanes)
    high, low = split(spread)
    r_high, r_low = split(right)
    return dot_nt(
        jnp.concatenate([high, low, high], axis=1),
        jnp.concatenate([r_high, r_high, r_low], axis=1),
    )


def momentum_kernel(momentum_ref, coeffs_ref, left_ref, right_ref, out_ref):
    own = encode(decay_rate * momentum_ref[0], left_ref[...], right_ref[...])
    out_ref[...] = own + jnp.sum(coeffs_ref[...], axis=0)


def plane_coeffs(momentum, coeffs, left, right):
    return pl.pallas_call(
        momentum_kernel,
        out_shape=jax.ShapeDtypeStruct(coeffs.shape[1:], f32),
        in_specs=whole(4),
        out_specs=pl.BlockSpec(memory_space=pltpu.VMEM),
        compiler_params=params(16),
        cost_estimate=COST,
    )(momentum, coeffs, left, right)


def update_kernel(coeffs_ref, left_ref, right_ref, out_ref):
    total = jnp.sum(coeffs_ref[...], axis=0)
    out_ref[...] = decode(total, left_ref[...], right_ref[...]).astype(bf16)


def decoded_update(coeffs, left, right, rows):
    return pl.pallas_call(
        update_kernel,
        out_shape=jax.ShapeDtypeStruct((rows, right.shape[0]), bf16),
        in_specs=whole(3),
        out_specs=pl.BlockSpec(memory_space=pltpu.VMEM),
        compiler_params=params(16),
        cost_estimate=COST,
    )(coeffs, left, right)


def half_gradient(refs, side, columns):
    lanes = slice(side * columns, (side + 1) * columns)
    blocks = partial(refs[:SIDE], 0, lanes)
    depth = blocks[0].shape[0]
    for q, block in enumerate(blocks):
        for r in range(0, depth, BAND):
            total = block[r : r + BAND]
            for ref in refs[SIDE:]:
                total = total + decoded(ref, q * depth + r, lanes)
            yield q * depth + r, total


def other_kernel(*refs):
    *in_refs, out_ref = refs
    for r, total in half_gradient(in_refs, 1, out_ref.shape[1]):
        out_ref[r : r + BAND, :] = total


def other_half(packets, coded):
    return pl.pallas_call(
        other_kernel,
        out_shape=jax.ShapeDtypeStruct((coded[0].shape[0] - 16, coded[0].shape[1] // 2), f32),
        in_specs=whole(len(packets) + len(coded)),
        out_specs=pl.BlockSpec(memory_space=pltpu.VMEM),
        compiler_params=params(16),
        cost_estimate=COST,
    )(*packets, *coded)


def fresh_kernel(*refs):
    *in_refs, momentum_ref, out_ref = refs
    for r, total in half_gradient(in_refs, 0, out_ref.shape[1]):
        out_ref[r : r + BAND, :] = decay_rate * momentum_ref[0, r : r + BAND, :] + total


def own_fresh(packets, coded, momentum):
    return pl.pallas_call(
        fresh_kernel,
        out_shape=jax.ShapeDtypeStruct(momentum.shape[1:], f32),
        in_specs=whole(len(packets) + len(coded) + 1),
        out_specs=pl.BlockSpec(memory_space=pltpu.VMEM),
        compiler_params=params(16),
        cost_estimate=COST,
    )(*packets, *coded, momentum)


def residual_kernel(own_ref, other_ref, left_ref, right_ref, out_ref):
    fresh = own_ref[...] + other_ref[...]
    left, right = left_ref[...], right_ref[...]
    out_ref[0] = fresh - decode(encode(fresh, left, right), left, right)


def residual_of(own, other, left, right):
    return pl.pallas_call(
        residual_kernel,
        out_shape=jax.ShapeDtypeStruct((1,) + own.shape, f32),
        in_specs=whole(4),
        out_specs=pl.BlockSpec(memory_space=pltpu.VMEM),
        compiler_params=params(16),
        cost_estimate=COST,
    )(own, other, left, right)


def spot(y, x, core):
    return ((y % SIDE) * SIDE + x % SIDE) * 2 + core


def shifted(block, step, phase):
    pairs = []
    for y in range(SIDE):
        for x in range(SIDE):
            for core in range(2):
                along_x = core == phase
                to = spot(y, x + step, core) if along_x else spot(y + step, x, core)
                pairs.append((spot(y, x, core), to))
    return lax.ppermute(block, "shard", pairs)


def on_device(hidden_acts, out_grads, momentum, kept):
    tok, rows = hidden_acts.shape
    columns = momentum.shape[2]
    shards = out_grads.shape[1] // columns
    replicas = lax.axis_size("rep")
    me = lax.axis_index("shard").astype(jnp.int32)

    packets, acts = first_packets(me, hidden_acts, out_grads)
    packets = [packets[0]] + [shifted(p, d, 0) for p, d in zip(packets[1:], OFFSETS[1:])]

    coeffs, left, right = local_coeffs(kept, cosine_table(), acts, out_grads, columns)

    coeffs = lax.all_to_all(coeffs, "shard", split_axis=0, concat_axis=0, tiled=True)
    coeffs, *packets = lax.optimization_barrier((coeffs, *packets))

    near = coded_partials(packets, NEAR[1:])
    coded = [shifted(c, OFFSETS[j], 1) for c, j in zip(near, NEAR[1:])]
    near, packets = lax.optimization_barrier((near, packets))
    (far,) = coded_partials(packets, (FAR,))
    coded.append(shifted(far, OFFSETS[FAR], 1))

    coeffs = plane_coeffs(momentum, coeffs, left, right)
    coeffs = lax.all_to_all(
        jnp.broadcast_to(coeffs[None], (replicas,) + coeffs.shape),
        "rep",
        split_axis=0,
        concat_axis=0,
        tiled=True,
    )
    coeffs, packets, coded = lax.optimization_barrier((coeffs, packets, coded))
    update = decoded_update(coeffs, left, right, rows)

    other = other_half(packets, coded)
    swap = [(i, i ^ 1) for i in range(shards)]
    other = lax.ppermute(other, "shard", swap)
    own = own_fresh(packets, coded, momentum)
    residual = residual_of(own, other, left, right)
    return (residual, update)


def solution(mesh):
    placed = (P(("rep", "shard"), None), P(("rep", "shard"), None), P("rep", None, "shard"), P())
    return jax.shard_map(
        on_device,
        mesh=mesh,
        in_specs=placed,
        out_specs=(P("rep", None, "shard"), P(None, "shard")),
        check_vma=False,
    )
```

```python
import functools
import math

import jax
import jax.numpy as jnp
import numpy as np
from jax import lax
from jax.experimental import pallas as pl
from jax.experimental.pallas import tpu as pltpu
from jax.sharding import PartitionSpec as P

GROUP = 64
KEPT = 32
SIDE = 4
CHIPS = SIDE * SIDE
OFFSETS = (0, 2, 1, -1)
FAR, NEAR = 1, (0, 2, 3)

decay_rate = 0.9
f32 = jnp.float32
bf16 = jnp.bfloat16
HIGHEST = lax.Precision.HIGHEST
MIB = 1 << 20
COST = pl.CostEstimate(flops=0, bytes_accessed=0, transcendentals=0)


def dot(a, b, precision=None):
    return jnp.dot(a, b, preferred_element_type=f32, precision=precision)


def dot_nt(a, b, precision=None):
    return lax.dot_general(
        a, b, (((1,), (1,)), ((), ())), preferred_element_type=f32, precision=precision
    )


def whole(n):
    return [pl.BlockSpec(memory_space=pltpu.VMEM)] * n


def params(mib=48):
    return pltpu.CompilerParams(vmem_limit_bytes=mib * MIB)


def place_of(me):
    core, x, y = me % 2, me // 2 % SIDE, me // (2 * SIDE)
    return core, jnp.where(core == 0, x, y), jnp.where(core == 0, y, x)


def gradient_parts(me, i, width):
    core, near, far = place_of(me)
    a = (near + OFFSETS[i] + SIDE) % SIDE
    for j, d in enumerate(OFFSETS):
        b = (far + d + SIDE) % SIDE
        chip = jnp.where(core == 0, b * SIDE + a, a * SIDE + b)
        for h in range(2):
            yield j, h, pl.multiple_of(chip * width + (core + h) % 2 * (width // 2), width // 2)


def far_kernel(me_ref, acts_hbm, grads_hbm, out_ref, acts_ref, sem, sems):
    tok, rows = acts_ref.shape
    width = out_ref.shape[1]
    depth = rows * tok // width
    half = width // 2
    copies = [pltpu.make_async_copy(acts_hbm, acts_ref, sem)]
    for j, h, start in gradient_parts(me_ref[0], FAR, width):
        copies.append(
            pltpu.make_async_copy(
                grads_hbm.at[:, pl.ds(start, half)],
                out_ref.at[depth + j * tok : depth + (j + 1) * tok, h * half : (h + 1) * half],
                sems.at[len(copies) - 1],
            )
        )
    for copy in copies:
        copy.start()
    copies[0].wait()
    acts_t = acts_ref[...].astype(f32).T.astype(bf16)
    for q in range(width // tok):
        out_ref[0:depth, q * tok : (q + 1) * tok] = acts_t[q * depth : (q + 1) * depth]
    for copy in copies[1:]:
        copy.wait()


def near_kernel(me_ref, far_ref, grads_ref, *out_refs):
    tok = grads_ref.shape[0]
    length, width = far_ref.shape
    depth = length - SIDE * tok
    half = width // 2
    for i, ref in zip(NEAR, out_refs):
        ref[0:depth, :] = far_ref[0:depth, :]
        for j, h, start in gradient_parts(me_ref[0], i, width):
            ref[depth + j * tok : depth + (j + 1) * tok, h * half : (h + 1) * half] = grads_ref[
                :, pl.ds(start, half)
            ]


def first_packets(me, acts, grads):
    tok, rows = acts.shape
    width = grads.shape[1] // CHIPS
    packet = jax.ShapeDtypeStruct((rows * tok // width + SIDE * tok, width), bf16)
    far, held = pl.pallas_call(
        far_kernel,
        out_shape=(packet, jax.ShapeDtypeStruct(acts.shape, acts.dtype)),
        in_specs=[pl.BlockSpec(memory_space=pltpu.SMEM)]
        + [pl.BlockSpec(memory_space=pltpu.HBM)] * 2,
        out_specs=tuple(whole(2)),
        scratch_shapes=[pltpu.SemaphoreType.DMA, pltpu.SemaphoreType.DMA((2 * SIDE,))],
        compiler_params=params(16),
        cost_estimate=COST,
    )(me[None], *(pltpu.with_memory_space_constraint(a, pltpu.HBM) for a in (acts, grads)))
    near = pl.pallas_call(
        near_kernel,
        out_shape=(packet,) * len(NEAR),
        in_specs=[pl.BlockSpec(memory_space=pltpu.SMEM)] + whole(2),
        out_specs=tuple(whole(len(NEAR))),
        compiler_params=params(16),
        cost_estimate=COST,
    )(me[None], far, grads)
    return [near[0], far, near[1], near[2]], held


def second_kernel(*refs):
    in_refs, out_refs = refs[:SIDE], refs[SIDE:]
    length, width = out_refs[0].shape
    tok = width // SIDE
    rows = length - SIDE * tok
    depth = rows * tok // width
    for i, ref in enumerate(in_refs):
        for q in range(SIDE):
            quarter = ref[0:depth, q * tok : (q + 1) * tok]
            for out_ref in out_refs:
                out_ref[q * depth : (q + 1) * depth, i * tok : (i + 1) * tok] = quarter
        for j, out_ref in zip(NEAR, out_refs):
            out_ref[rows + i * tok : rows + (i + 1) * tok, :] = ref[
                depth + j * tok : depth + (j + 1) * tok, :
            ]


def second_packets(packets, rows):
    length, width = packets[0].shape
    packet = jax.ShapeDtypeStruct((rows + width, width), bf16)
    return pl.pallas_call(
        second_kernel,
        out_shape=(packet,) * len(NEAR),
        in_specs=whole(SIDE),
        out_specs=tuple(whole(len(NEAR))),
        compiler_params=params(16),
        cost_estimate=COST,
    )(*packets)


BAND = 128
MARGIN = 0.998


def partial(refs, j):
    length, width = refs[0].shape
    tok = width // SIDE
    depth = length - SIDE * tok
    grads = jnp.concatenate(
        [ref[depth + j * tok : depth + (j + 1) * tok, :] for ref in refs], axis=0
    )
    blocks = []
    for q in range(SIDE):
        acts = jnp.concatenate([ref[0:depth, q * tok : (q + 1) * tok] for ref in refs], axis=1)
        blocks.append(dot(acts, grads))
    return blocks


def coded_kernel(j, *refs):
    *packet_refs, out_ref = refs
    blocks = partial(packet_refs, j)
    depth, width = blocks[0].shape
    exponents = []
    for q, block in enumerate(blocks):
        for r in range(0, depth, BAND):
            values = block[r : r + BAND]
            largest = jnp.max(jnp.abs(values), axis=0, keepdims=True)
            exponent = jnp.floor(jnp.log2(jnp.maximum(largest, 1e-30))) + 1.0
            scaled = jnp.round(values * (MARGIN * jnp.exp2(15.0 - exponent)))
            start = q * depth + r
            out_ref[start : start + BAND, :] = scaled.astype(jnp.int32).astype(jnp.int16)
            exponents.append(exponent)
    exponents = jnp.concatenate(exponents + [jnp.zeros_like(exponents[0])] * 8, axis=0)
    out_ref[SIDE * depth :, :] = exponents.astype(jnp.int32).astype(jnp.int16)


def coded_partial(packets, j):
    length, width = packets[0].shape
    rows = SIDE * (length - width)
    return pl.pallas_call(
        functools.partial(coded_kernel, j),
        out_shape=jax.ShapeDtypeStruct((rows + 16, width), jnp.int16),
        in_specs=whole(SIDE),
        out_specs=pl.BlockSpec(memory_space=pltpu.VMEM),
        compiler_params=params(16),
        cost_estimate=COST,
    )(*packets)


def decoded(ref, r, lanes):
    rows = ref.shape[0] - 16
    exponent = ref[rows:, lanes].astype(jnp.int32).astype(f32)[r // BAND : r // BAND + 1]
    return ref[r : r + BAND, lanes].astype(jnp.int32).astype(f32) * (jnp.exp2(exponent - 15.0) / MARGIN)


def split(a):
    high = a.astype(bf16)
    return high, (a - high.astype(f32)).astype(bf16)


def split3(a):
    high = a.astype(bf16)
    rest = a - high.astype(f32)
    middle = rest.astype(bf16)
    return high, middle, (rest - middle.astype(f32)).astype(bf16)


BATCH = 8


def coeff_kernel(kept_ref, table_ref, acts_ref, grads_ref, out_ref, left_ref, right_ref, twice_ref):
    tok, rows = acts_ref.shape
    bands = rows // GROUP
    groups, _, lanes = out_ref.shape
    columns = right_ref.shape[0]

    frequency = lax.broadcasted_iota(jnp.int32, (GROUP, lanes), 0)
    table = table_ref[...]
    kept_lanes = jnp.concatenate([kept_ref[...]] * (lanes // KEPT), axis=1)
    picked_row = jnp.where(frequency == kept_lanes // GROUP, 1.0, 0.0)
    picked_column = jnp.where(frequency == kept_lanes % GROUP, 1.0, 0.0)
    left = dot(table, picked_row, HIGHEST)
    tall = dot(table, picked_column, HIGHEST)
    left_ref[...] = left
    lane = lax.broadcasted_iota(jnp.int32, (GROUP, lanes), 1)
    right = jnp.concatenate(
        [jnp.where(lane // KEPT == b, tall, 0.0) for b in range(columns // GROUP)], axis=0
    )
    right_ref[...] = right
    pieces = jnp.concatenate(split(right), axis=1)

    acts_t = acts_ref[...].astype(f32).T.astype(bf16)
    twice_ref[:, 0:tok] = acts_t
    twice_ref[:, tok : 2 * tok] = acts_t

    def step(i, carry):
        start = pl.multiple_of(i * BATCH * columns, BATCH * columns)
        grads = jnp.concatenate(
            [grads_ref[:, pl.ds(start + j * columns, columns)] for j in range(BATCH)], axis=0
        )
        moved = dot(grads, pieces)
        high, low = split(moved[:, :lanes] + moved[:, lanes:])
        for j in range(0, BATCH, 2):
            both = [jnp.concatenate([p[m * tok : (m + 1) * tok] for p in (high, low)], axis=0) for m in (j, j + 1)]
            product = dot(twice_ref[...], jnp.concatenate(both, axis=1))
            for m in range(2):
                part = product[:, m * lanes : (m + 1) * lanes].reshape(bands, GROUP, lanes) * left[None]
                out_ref[pl.ds(i * BATCH + j + m, 1)] = jnp.sum(part, axis=1)[None]
        return carry

    lax.fori_loop(0, groups // BATCH, step, 0, unroll=groups // BATCH)


def cosine_table():
    frequency = np.arange(GROUP, dtype=np.float32)[None, :]
    position = np.arange(GROUP, dtype=np.float32)[:, None]
    table = np.cos(
        np.float32(math.pi) * (2.0 * position + 1.0) * frequency / np.float32(2.0 * GROUP)
    ) * np.float32(math.sqrt(2.0 / GROUP))
    table = (table * np.where(frequency == 0.0, math.sqrt(0.5), 1.0)).astype(np.float32)
    return jnp.asarray(table)


def local_coeffs(kept, table, acts, grads, columns):
    tok, rows = acts.shape
    bands = rows // GROUP
    lanes = columns // GROUP * KEPT
    return pl.pallas_call(
        coeff_kernel,
        out_shape=(
            jax.ShapeDtypeStruct((grads.shape[1] // columns, bands, lanes), f32),
            jax.ShapeDtypeStruct((GROUP, lanes), f32),
            jax.ShapeDtypeStruct((columns, lanes), f32),
        ),
        in_specs=whole(4),
        out_specs=tuple(whole(3)),
        scratch_shapes=[pltpu.VMEM((rows, 2 * tok), bf16)],
        compiler_params=params(16),
        cost_estimate=COST,
    )(kept[None, :], table, acts, grads)


def encode(field, left, right):
    rows = field.shape[0]
    high, low = split(field)
    r_high, r_low = split(right)
    lanes = right.shape[1]
    moved = dot(high, jnp.concatenate([r_high, r_low], axis=1))
    moved = moved[:, :lanes] + (moved[:, lanes:] + dot(low, r_high))
    moved = moved.reshape(rows // GROUP, GROUP, right.shape[1]) * left[None]
    return jnp.sum(moved, axis=1)


def decode(coeffs, left, right):
    bands, lanes = coeffs.shape
    spread = (coeffs[:, None, :] * left[None]).reshape(bands * GROUP, lanes)
    high, low = split(spread)
    r_high, r_low = split(right)
    return dot_nt(
        jnp.concatenate([high, low, high], axis=1),
        jnp.concatenate([r_high, r_high, r_low], axis=1),
    )


def momentum_kernel(momentum_ref, coeffs_ref, left_ref, right_ref, out_ref):
    own = encode(decay_rate * momentum_ref[0], left_ref[...], right_ref[...])
    out_ref[...] = own + jnp.sum(coeffs_ref[...], axis=0)


def plane_coeffs(momentum, coeffs, left, right):
    return pl.pallas_call(
        momentum_kernel,
        out_shape=jax.ShapeDtypeStruct(coeffs.shape[1:], f32),
        in_specs=whole(4),
        out_specs=pl.BlockSpec(memory_space=pltpu.VMEM),
        compiler_params=params(16),
        cost_estimate=COST,
    )(momentum, coeffs, left, right)


def update_kernel(coeffs_ref, left_ref, right_ref, out_ref):
    total = jnp.sum(coeffs_ref[...], axis=0)
    out_ref[...] = decode(total, left_ref[...], right_ref[...]).astype(bf16)


def decoded_update(coeffs, left, right, rows):
    return pl.pallas_call(
        update_kernel,
        out_shape=jax.ShapeDtypeStruct((rows, right.shape[0]), bf16),
        in_specs=whole(3),
        out_specs=pl.BlockSpec(memory_space=pltpu.VMEM),
        compiler_params=params(16),
        cost_estimate=COST,
    )(coeffs, left, right)


def half_gradient(packet_refs, coded_ref, side, columns):
    lanes = slice(side * columns, (side + 1) * columns)
    total = None
    for ref in packet_refs:
        rows = ref.shape[0] - ref.shape[1]
        term = dot(ref[0:rows, :], ref[rows:, lanes])
        total = term if total is None else total + term
    for r in range(0, total.shape[0], BAND):
        yield r, total[r : r + BAND] + decoded(coded_ref, r, lanes)


def other_kernel(*refs):
    *packet_refs, coded_ref, out_ref = refs
    for r, total in half_gradient(packet_refs, coded_ref, 1, out_ref.shape[1]):
        out_ref[r : r + BAND, :] = total


def other_half(packets, coded):
    length, width = packets[0].shape
    return pl.pallas_call(
        other_kernel,
        out_shape=jax.ShapeDtypeStruct((length - width, width // 2), f32),
        in_specs=whole(len(packets) + 1),
        out_specs=pl.BlockSpec(memory_space=pltpu.VMEM),
        compiler_params=params(16),
        cost_estimate=COST,
    )(*packets, coded)


def fresh_kernel(*refs):
    *packet_refs, coded_ref, momentum_ref, out_ref = refs
    for r, total in half_gradient(packet_refs, coded_ref, 0, out_ref.shape[1]):
        out_ref[r : r + BAND, :] = decay_rate * momentum_ref[0, r : r + BAND, :] + total


def own_fresh(packets, coded, momentum):
    return pl.pallas_call(
        fresh_kernel,
        out_shape=jax.ShapeDtypeStruct(momentum.shape[1:], f32),
        in_specs=whole(len(packets) + 2),
        out_specs=pl.BlockSpec(memory_space=pltpu.VMEM),
        compiler_params=params(16),
        cost_estimate=COST,
    )(*packets, coded, momentum)


def residual_kernel(own_ref, other_ref, left_ref, right_ref, out_ref):
    fresh = own_ref[...] + other_ref[...]
    left, right = left_ref[...], right_ref[...]
    out_ref[0] = fresh - decode(encode(fresh, left, right), left, right)


def residual_of(own, other, left, right):
    return pl.pallas_call(
        residual_kernel,
        out_shape=jax.ShapeDtypeStruct((1,) + own.shape, f32),
        in_specs=whole(4),
        out_specs=pl.BlockSpec(memory_space=pltpu.VMEM),
        compiler_params=params(16),
        cost_estimate=COST,
    )(own, other, left, right)


def spot(y, x, core):
    return ((y % SIDE) * SIDE + x % SIDE) * 2 + core


def shifted(block, step, phase):
    pairs = []
    for y in range(SIDE):
        for x in range(SIDE):
            for core in range(2):
                along_x = core == phase
                to = spot(y, x + step, core) if along_x else spot(y + step, x, core)
                pairs.append((spot(y, x, core), to))
    return lax.ppermute(block, "shard", pairs)


def on_device(hidden_acts, out_grads, momentum, kept):
    tok, rows = hidden_acts.shape
    columns = momentum.shape[2]
    shards = out_grads.shape[1] // columns
    replicas = lax.axis_size("rep")
    me = lax.axis_index("shard").astype(jnp.int32)

    packets, acts = first_packets(me, hidden_acts, out_grads)
    packets = [packets[0]] + [shifted(p, d, 0) for p, d in zip(packets[1:], OFFSETS[1:])]

    coeffs, left, right = local_coeffs(kept, cosine_table(), acts, out_grads, columns)

    coeffs = lax.all_to_all(coeffs, "shard", split_axis=0, concat_axis=0, tiled=True)
    coeffs, *packets = lax.optimization_barrier((coeffs, *packets))

    coded = shifted(coded_partial(packets, FAR), OFFSETS[FAR], 1)
    packets = second_packets(packets, rows)
    packets = [packets[0]] + [shifted(p, OFFSETS[j], 1) for p, j in zip(packets[1:], NEAR[1:])]

    coeffs = plane_coeffs(momentum, coeffs, left, right)
    coeffs = lax.all_to_all(
        jnp.broadcast_to(coeffs[None], (replicas,) + coeffs.shape),
        "rep",
        split_axis=0,
        concat_axis=0,
        tiled=True,
    )
    coeffs, coded, *packets = lax.optimization_barrier((coeffs, coded, *packets))
    update = decoded_update(coeffs, left, right, rows)

    other = other_half(packets, coded)
    swap = [(i, i ^ 1) for i in range(shards)]
    other = lax.ppermute(other, "shard", swap)
    own = own_fresh(packets, coded, momentum)
    residual = residual_of(own, other, left, right)
    return (residual, update)


def solution(mesh):
    placed = (P(("rep", "shard"), None), P(("rep", "shard"), None), P("rep", None, "shard"), P())
    return jax.shard_map(
        on_device,
        mesh=mesh,
        in_specs=placed,
        out_specs=(P("rep", None, "shard"), P(None, "shard")),
        check_vma=False,
    )
```

```python
import functools
import math

import jax
import jax.numpy as jnp
import numpy as np
from jax import lax
from jax.experimental import pallas as pl
from jax.experimental.pallas import tpu as pltpu
from jax.sharding import PartitionSpec as P

GROUP = 64
KEPT = 32
SIDE = 4
CHIPS = SIDE * SIDE
OFFSETS = (0, 2, 1, -1)
FAR, NEAR = 1, (0, 2, 3)

decay_rate = 0.9
f32 = jnp.float32
bf16 = jnp.bfloat16
HIGHEST = lax.Precision.HIGHEST
MIB = 1 << 20
COST = pl.CostEstimate(flops=0, bytes_accessed=0, transcendentals=0)


def dot(a, b, precision=None):
    return jnp.dot(a, b, preferred_element_type=f32, precision=precision)


def dot_nt(a, b, precision=None):
    return lax.dot_general(
        a, b, (((1,), (1,)), ((), ())), preferred_element_type=f32, precision=precision
    )


def whole(n):
    return [pl.BlockSpec(memory_space=pltpu.VMEM)] * n


def params(mib=48):
    return pltpu.CompilerParams(vmem_limit_bytes=mib * MIB)


def place_of(me):
    core, x, y = me % 2, me // 2 % SIDE, me // (2 * SIDE)
    return core, jnp.where(core == 0, x, y), jnp.where(core == 0, y, x)


def gradient_parts(me, i, width):
    core, near, far = place_of(me)
    a = (near + OFFSETS[i] + SIDE) % SIDE
    for j, d in enumerate(OFFSETS):
        b = (far + d + SIDE) % SIDE
        chip = jnp.where(core == 0, b * SIDE + a, a * SIDE + b)
        for h in range(2):
            yield j, h, pl.multiple_of(chip * width + (core + h) % 2 * (width // 2), width // 2)


def far_kernel(me_ref, acts_hbm, grads_hbm, out_ref, acts_ref, sem, sems):
    tok, rows = acts_ref.shape
    width = out_ref.shape[1]
    depth = rows * tok // width
    half = width // 2
    copies = [pltpu.make_async_copy(acts_hbm, acts_ref, sem)]
    for j, h, start in gradient_parts(me_ref[0], FAR, width):
        copies.append(
            pltpu.make_async_copy(
                grads_hbm.at[:, pl.ds(start, half)],
                out_ref.at[depth + j * tok : depth + (j + 1) * tok, h * half : (h + 1) * half],
                sems.at[len(copies) - 1],
            )
        )
    for copy in copies:
        copy.start()
    copies[0].wait()
    acts_t = acts_ref[...].astype(f32).T.astype(bf16)
    for q in range(width // tok):
        out_ref[0:depth, q * tok : (q + 1) * tok] = acts_t[q * depth : (q + 1) * depth]
    for copy in copies[1:]:
        copy.wait()


def near_kernel(me_ref, far_ref, grads_ref, *out_refs):
    tok = grads_ref.shape[0]
    length, width = far_ref.shape
    depth = length - SIDE * tok
    half = width // 2
    for i, ref in zip(NEAR, out_refs):
        ref[0:depth, :] = far_ref[0:depth, :]
        for j, h, start in gradient_parts(me_ref[0], i, width):
            ref[depth + j * tok : depth + (j + 1) * tok, h * half : (h + 1) * half] = grads_ref[
                :, pl.ds(start, half)
            ]


def first_packets(me, acts, grads):
    tok, rows = acts.shape
    width = grads.shape[1] // CHIPS
    packet = jax.ShapeDtypeStruct((rows * tok // width + SIDE * tok, width), bf16)
    far, held = pl.pallas_call(
        far_kernel,
        out_shape=(packet, jax.ShapeDtypeStruct(acts.shape, acts.dtype)),
        in_specs=[pl.BlockSpec(memory_space=pltpu.SMEM)]
        + [pl.BlockSpec(memory_space=pltpu.HBM)] * 2,
        out_specs=tuple(whole(2)),
        scratch_shapes=[pltpu.SemaphoreType.DMA, pltpu.SemaphoreType.DMA((2 * SIDE,))],
        compiler_params=params(16),
        cost_estimate=COST,
    )(me[None], *(pltpu.with_memory_space_constraint(a, pltpu.HBM) for a in (acts, grads)))
    near = pl.pallas_call(
        near_kernel,
        out_shape=(packet,) * len(NEAR),
        in_specs=[pl.BlockSpec(memory_space=pltpu.SMEM)] + whole(2),
        out_specs=tuple(whole(len(NEAR))),
        compiler_params=params(16),
        cost_estimate=COST,
    )(me[None], far, grads)
    return [near[0], far, near[1], near[2]], held


def second_kernel(*refs):
    in_refs, out_refs = refs[:SIDE], refs[SIDE:]
    length, width = out_refs[0].shape
    tok = width // SIDE
    rows = length - SIDE * tok
    depth = rows * tok // width
    for i, ref in enumerate(in_refs):
        for q in range(SIDE):
            quarter = ref[0:depth, q * tok : (q + 1) * tok]
            for out_ref in out_refs:
                out_ref[q * depth : (q + 1) * depth, i * tok : (i + 1) * tok] = quarter
        for j, out_ref in zip(NEAR, out_refs):
            out_ref[rows + i * tok : rows + (i + 1) * tok, :] = ref[
                depth + j * tok : depth + (j + 1) * tok, :
            ]


def second_packets(packets, rows):
    length, width = packets[0].shape
    packet = jax.ShapeDtypeStruct((rows + width, width), bf16)
    return pl.pallas_call(
        second_kernel,
        out_shape=(packet,) * len(NEAR),
        in_specs=whole(SIDE),
        out_specs=tuple(whole(len(NEAR))),
        compiler_params=params(16),
        cost_estimate=COST,
    )(*packets)


BAND = 128
MARGIN = 0.998


def partial(refs, j):
    length, width = refs[0].shape
    tok = width // SIDE
    depth = length - SIDE * tok
    grads = jnp.concatenate(
        [ref[depth + j * tok : depth + (j + 1) * tok, :] for ref in refs], axis=0
    )
    blocks = []
    for q in range(SIDE):
        acts = jnp.concatenate([ref[0:depth, q * tok : (q + 1) * tok] for ref in refs], axis=1)
        blocks.append(dot(acts, grads))
    return blocks


def coded_kernel(j, *refs):
    *packet_refs, out_ref = refs
    blocks = partial(packet_refs, j)
    depth, width = blocks[0].shape
    exponents = []
    for q, block in enumerate(blocks):
        for r in range(0, depth, BAND):
            values = block[r : r + BAND]
            largest = jnp.max(jnp.abs(values), axis=0, keepdims=True)
            exponent = jnp.floor(jnp.log2(jnp.maximum(largest, 1e-30))) + 1.0
            scaled = jnp.round(values * (MARGIN * jnp.exp2(15.0 - exponent)))
            start = q * depth + r
            out_ref[start : start + BAND, :] = scaled.astype(jnp.int32).astype(jnp.int16)
            exponents.append(exponent)
    exponents = jnp.concatenate(exponents + [jnp.zeros_like(exponents[0])] * 8, axis=0)
    out_ref[SIDE * depth :, :] = exponents.astype(jnp.int32).astype(jnp.int16)


def coded_partial(packets, j):
    length, width = packets[0].shape
    rows = SIDE * (length - width)
    return pl.pallas_call(
        functools.partial(coded_kernel, j),
        out_shape=jax.ShapeDtypeStruct((rows + 16, width), jnp.int16),
        in_specs=whole(SIDE),
        out_specs=pl.BlockSpec(memory_space=pltpu.VMEM),
        compiler_params=params(16),
        cost_estimate=COST,
    )(*packets)


def decoded(ref, r, lanes):
    rows = ref.shape[0] - 16
    exponent = ref[rows:, lanes].astype(jnp.int32).astype(f32)[r // BAND : r // BAND + 1]
    return ref[r : r + BAND, lanes].astype(jnp.int32).astype(f32) * (jnp.exp2(exponent - 15.0) / MARGIN)


def split(a):
    high = a.astype(bf16)
    return high, (a - high.astype(f32)).astype(bf16)


def split3(a):
    high = a.astype(bf16)
    rest = a - high.astype(f32)
    middle = rest.astype(bf16)
    return high, middle, (rest - middle.astype(f32)).astype(bf16)


BATCH = 8


def coeff_kernel(
    kept_ref, table_ref, acts_ref, grads_ref, momentum_ref,
    out_ref, left_ref, right_ref, momentum_out_ref, twice_ref,
):
    tok, rows = acts_ref.shape
    bands = rows // GROUP
    groups, _, lanes = out_ref.shape
    columns = right_ref.shape[0]

    frequency = lax.broadcasted_iota(jnp.int32, (GROUP, lanes), 0)
    table = table_ref[...]
    kept_lanes = jnp.concatenate([kept_ref[...]] * (lanes // KEPT), axis=1)
    picked_row = jnp.where(frequency == kept_lanes // GROUP, 1.0, 0.0)
    picked_column = jnp.where(frequency == kept_lanes % GROUP, 1.0, 0.0)
    left = dot(table, picked_row, HIGHEST)
    tall = dot(table, picked_column, HIGHEST)
    left_ref[...] = left
    lane = lax.broadcasted_iota(jnp.int32, (GROUP, lanes), 1)
    right = jnp.concatenate(
        [jnp.where(lane // KEPT == b, tall, 0.0) for b in range(columns // GROUP)], axis=0
    )
    right_ref[...] = right
    momentum_out_ref[...] = encode(decay_rate * momentum_ref[0], left, right)
    pieces = jnp.concatenate(split(right), axis=1)

    acts_t = acts_ref[...].astype(f32).T.astype(bf16)
    twice_ref[:, 0:tok] = acts_t
    twice_ref[:, tok : 2 * tok] = acts_t

    def step(i, carry):
        start = pl.multiple_of(i * BATCH * columns, BATCH * columns)
        grads = jnp.concatenate(
            [grads_ref[:, pl.ds(start + j * columns, columns)] for j in range(BATCH)], axis=0
        )
        moved = dot(grads, pieces)
        high, low = split(moved[:, :lanes] + moved[:, lanes:])
        for j in range(0, BATCH, 2):
            both = [jnp.concatenate([p[m * tok : (m + 1) * tok] for p in (high, low)], axis=0) for m in (j, j + 1)]
            product = dot(twice_ref[...], jnp.concatenate(both, axis=1))
            for m in range(2):
                part = product[:, m * lanes : (m + 1) * lanes].reshape(bands, GROUP, lanes) * left[None]
                out_ref[pl.ds(i * BATCH + j + m, 1)] = jnp.sum(part, axis=1)[None]
        return carry

    lax.fori_loop(0, groups // BATCH, step, 0, unroll=groups // BATCH)


def cosine_table():
    frequency = np.arange(GROUP, dtype=np.float32)[None, :]
    position = np.arange(GROUP, dtype=np.float32)[:, None]
    table = np.cos(
        np.float32(math.pi) * (2.0 * position + 1.0) * frequency / np.float32(2.0 * GROUP)
    ) * np.float32(math.sqrt(2.0 / GROUP))
    table = (table * np.where(frequency == 0.0, math.sqrt(0.5), 1.0)).astype(np.float32)
    return jnp.asarray(table)


def local_coeffs(kept, table, acts, grads, momentum):
    tok, rows = acts.shape
    bands = rows // GROUP
    columns = momentum.shape[2]
    lanes = columns // GROUP * KEPT
    return pl.pallas_call(
        coeff_kernel,
        out_shape=(
            jax.ShapeDtypeStruct((grads.shape[1] // columns, bands, lanes), f32),
            jax.ShapeDtypeStruct((GROUP, lanes), f32),
            jax.ShapeDtypeStruct((columns, lanes), f32),
            jax.ShapeDtypeStruct((bands, lanes), f32),
        ),
        in_specs=whole(5),
        out_specs=tuple(whole(4)),
        scratch_shapes=[pltpu.VMEM((rows, 2 * tok), bf16)],
        compiler_params=params(16),
        cost_estimate=COST,
    )(kept[None, :], table, acts, grads, momentum)


def encode(field, left, right):
    rows = field.shape[0]
    high, low = split(field)
    r_high, r_low = split(right)
    lanes = right.shape[1]
    moved = dot(high, jnp.concatenate([r_high, r_low], axis=1))
    moved = moved[:, :lanes] + (moved[:, lanes:] + dot(low, r_high))
    moved = moved.reshape(rows // GROUP, GROUP, right.shape[1]) * left[None]
    return jnp.sum(moved, axis=1)


def decode(coeffs, left, right):
    bands, lanes = coeffs.shape
    spread = (coeffs[:, None, :] * left[None]).reshape(bands * GROUP, lanes)
    high, low = split(spread)
    r_high, r_low = split(right)
    return dot_nt(
        jnp.concatenate([high, low, high], axis=1),
        jnp.concatenate([r_high, r_high, r_low], axis=1),
    )


def plane_kernel(own_ref, coeffs_ref, out_ref):
    out_ref[...] = own_ref[...] + jnp.sum(coeffs_ref[...], axis=0)


def plane_coeffs(own, coeffs):
    return pl.pallas_call(
        plane_kernel,
        out_shape=jax.ShapeDtypeStruct(own.shape, f32),
        in_specs=whole(2),
        out_specs=pl.BlockSpec(memory_space=pltpu.VMEM),
        compiler_params=params(16),
        cost_estimate=COST,
    )(own, coeffs)


def update_kernel(coeffs_ref, left_ref, right_ref, out_ref):
    total = jnp.sum(coeffs_ref[...], axis=0)
    out_ref[...] = decode(total, left_ref[...], right_ref[...]).astype(bf16)


def decoded_update(coeffs, left, right, rows):
    return pl.pallas_call(
        update_kernel,
        out_shape=jax.ShapeDtypeStruct((rows, right.shape[0]), bf16),
        in_specs=whole(3),
        out_specs=pl.BlockSpec(memory_space=pltpu.VMEM),
        compiler_params=params(16),
        cost_estimate=COST,
    )(coeffs, left, right)


def half_gradient(packet_refs, coded_ref, side, columns):
    lanes = slice(side * columns, (side + 1) * columns)
    total = None
    for ref in packet_refs:
        rows = ref.shape[0] - ref.shape[1]
        term = dot(ref[0:rows, :], ref[rows:, lanes])
        total = term if total is None else total + term
    for r in range(0, total.shape[0], BAND):
        yield r, total[r : r + BAND] + decoded(coded_ref, r, lanes)


def other_kernel(*refs):
    *packet_refs, coded_ref, out_ref = refs
    for r, total in half_gradient(packet_refs, coded_ref, 1, out_ref.shape[1]):
        out_ref[r : r + BAND, :] = total


def other_half(packets, coded):
    length, width = packets[0].shape
    return pl.pallas_call(
        other_kernel,
        out_shape=jax.ShapeDtypeStruct((length - width, width // 2), f32),
        in_specs=whole(len(packets) + 1),
        out_specs=pl.BlockSpec(memory_space=pltpu.VMEM),
        compiler_params=params(16),
        cost_estimate=COST,
    )(*packets, coded)


def fresh_kernel(*refs):
    *packet_refs, coded_ref, momentum_ref, out_ref = refs
    for r, total in half_gradient(packet_refs, coded_ref, 0, out_ref.shape[1]):
        out_ref[r : r + BAND, :] = decay_rate * momentum_ref[0, r : r + BAND, :] + total


def own_fresh(packets, coded, momentum):
    return pl.pallas_call(
        fresh_kernel,
        out_shape=jax.ShapeDtypeStruct(momentum.shape[1:], f32),
        in_specs=whole(len(packets) + 2),
        out_specs=pl.BlockSpec(memory_space=pltpu.VMEM),
        compiler_params=params(16),
        cost_estimate=COST,
    )(*packets, coded, momentum)


def residual_kernel(own_ref, other_ref, left_ref, right_ref, out_ref):
    fresh = own_ref[...] + other_ref[...]
    left, right = left_ref[...], right_ref[...]
    out_ref[0] = fresh - decode(encode(fresh, left, right), left, right)


def residual_of(own, other, left, right):
    return pl.pallas_call(
        residual_kernel,
        out_shape=jax.ShapeDtypeStruct((1,) + own.shape, f32),
        in_specs=whole(4),
        out_specs=pl.BlockSpec(memory_space=pltpu.VMEM),
        compiler_params=params(16),
        cost_estimate=COST,
    )(own, other, left, right)


def spot(y, x, core):
    return ((y % SIDE) * SIDE + x % SIDE) * 2 + core


def shifted(block, step, phase):
    pairs = []
    for y in range(SIDE):
        for x in range(SIDE):
            for core in range(2):
                along_x = core == phase
                to = spot(y, x + step, core) if along_x else spot(y + step, x, core)
                pairs.append((spot(y, x, core), to))
    return lax.ppermute(block, "shard", pairs)


def on_device(hidden_acts, out_grads, momentum, kept):
    tok, rows = hidden_acts.shape
    columns = momentum.shape[2]
    shards = out_grads.shape[1] // columns
    replicas = lax.axis_size("rep")
    me = lax.axis_index("shard").astype(jnp.int32)

    packets, acts = first_packets(me, hidden_acts, out_grads)
    packets = [packets[0]] + [shifted(p, d, 0) for p, d in zip(packets[1:], OFFSETS[1:])]

    coeffs, left, right, own_coeffs = local_coeffs(
        kept, cosine_table(), acts, out_grads, momentum
    )

    coeffs = lax.all_to_all(coeffs, "shard", split_axis=0, concat_axis=0, tiled=True)
    coeffs, *packets = lax.optimization_barrier((coeffs, *packets))

    coded = shifted(coded_partial(packets, FAR), OFFSETS[FAR], 1)
    packets = second_packets(packets, rows)
    packets = [packets[0]] + [shifted(p, OFFSETS[j], 1) for p, j in zip(packets[1:], NEAR[1:])]

    coeffs = plane_coeffs(own_coeffs, coeffs)
    coeffs = lax.all_to_all(
        jnp.broadcast_to(coeffs[None], (replicas,) + coeffs.shape),
        "rep",
        split_axis=0,
        concat_axis=0,
        tiled=True,
    )
    coeffs, coded, *packets = lax.optimization_barrier((coeffs, coded, *packets))
    update = decoded_update(coeffs, left, right, rows)

    other = other_half(packets, coded)
    swap = [(i, i ^ 1) for i in range(shards)]
    other = lax.ppermute(other, "shard", swap)
    own = own_fresh(packets, coded, momentum)
    residual = residual_of(own, other, left, right)
    return (residual, update)


def solution(mesh):
    placed = (P(("rep", "shard"), None), P(("rep", "shard"), None), P("rep", None, "shard"), P())
    return jax.shard_map(
        on_device,
        mesh=mesh,
        in_specs=placed,
        out_specs=(P("rep", None, "shard"), P(None, "shard")),
        check_vma=False,
    )
```
